32 devices in a mesh: seq: 4 (over y, x), fsdp: 8 (over z, core).
Axes of the slice: x: 2, y: 2, z: 4, core: 2. Of those that a mesh axis runs over, the one named last changes fastest.
Arguments:
- tokens: bfloat16 [8, 512, 768], P('fsdp', 'seq'), may hold values from -6 to 6
- cotangent: bfloat16 [8, 512, 768], P('fsdp', 'seq'), may hold values from -6 to 6
- w_qkv: bfloat16 [768, 2304], P('fsdp'), may hold values from -0.21875 to 0.21875
- w_attn_out: bfloat16 [768, 768], P('fsdp'), may hold values from -0.875 to 0.875
- w_in: bfloat16 [768, 2304], P('fsdp'), may hold values from -0.21875 to 0.21875
- w_mlp_out: bfloat16 [1152, 768], P(None, 'fsdp'), may hold values from -0.1875 to 0.1875
- gain_attn: bfloat16 [768], P('fsdp'), may hold values from 0.5 to 1.5
- gain_mlp: bfloat16 [768], P('fsdp'), may hold values from 0.5 to 1.5
Outputs:
- outputs: bfloat16 [8, 512, 768], P('fsdp', 'seq')
- grad_tokens: float32 [8, 512, 768], P('fsdp', 'seq')
- grad_qkv: float32 [768, 2304], P('fsdp')
- grad_attn_out: float32 [768, 768], P('fsdp')
- grad_in: float32 [768, 2304], P('fsdp')
- grad_mlp_out: float32 [1152, 768], P(None, 'fsdp')
- grad_gain_attn: float32 [768], P('fsdp')
- grad_gain_mlp: float32 [768], P('fsdp')
The draws below stay inside these ranges and needn't reach their ends.
All inputs are finite; a program needn't handle non-finite values.
Results may differ from the reference program's by a relative error of at most 0.017.
Values may be sent and summed in bfloat16 or wider, within the bound.
No kernel may reach another device: no remote copies, remote signals or barrier semaphores. Data moves between devices by JAX's collectives and lax.ppermute only.
A program may use at most 128 MiB of HBM per device.

```python
import math
import jax
import jax.numpy as jnp
from jax import lax

D = 768
HEADS = 12
FF = 1152
HALF = 64
LENGTH = 512
SEQS = 8


def spiked(array, stream_key, source, target, parts, factor):
    owner, partner = [(jnp.arange(array.shape[position]) // (array.shape[position] // parts)).reshape([-1 if axis == position else 1 for axis in range(array.ndim)]) for position in (source, target)]
    chosen = jax.random.permutation(stream_key, parts)[partner]
    strong = (owner == chosen) | (owner == (partner + parts // 2) % parts)
    return jnp.where(strong, factor * array, array)


def steps_of(key, dims, split, low, high):
    gain, own = 1.0, jax.random.fold_in(key, 6)
    for dim, blocks in split:
        heights = jnp.exp(jax.random.uniform(jax.random.fold_in(own, dim), (blocks,), jnp.float32, low / len(split), high / len(split)))
        gain = gain * jnp.repeat(heights, dims[dim] // blocks).reshape([-1 if axis == dim else 1 for axis in range(len(dims))])
    return gain


def normal_values(own_key, extent, deviation, bound, split=(), held_as=jnp.bfloat16):
    entries = jax.random.normal(own_key, extent, jnp.float32) * deviation
    if len(split) > 0:
        entries = steps_of(own_key, extent, split, -0.22, 0.18) * entries
    return jnp.clip(entries, min=-bound, max=bound).astype(held_as)


def noise_with(rng, extent, scale, most, pieces, heavy, kind=jnp.bfloat16):
    array = scale * jax.random.normal(rng, extent, jnp.float32)
    if pieces:
        array = array * steps_of(rng, extent, pieces, -0.22, 0.18)
    return jnp.clip(spiked(array, jax.random.fold_in(rng, 3), *heavy), -most, most).astype(kind)


def setup_inputs(seed: int = 0) -> dict:
    splits = jax.random.split(jax.random.key(seed), 9)
    tokens = normal_values(splits[0], (SEQS, LENGTH, D), 1.0, 6.0, ((0, 8), (1, 4)))
    cotangent = noise_with(splits[1], (SEQS, LENGTH, D), 1.0, 6.0, ((0, 8), (1, 4)), (0, 2, 8, 2.0))
    w_qkv = normal_values(splits[2], (D, 3 * D), D ** -0.5, 0.21875, ((0, 8),))
    w_attn_out = normal_values(splits[3], (D, D), (D // 16) ** -0.5, 0.875, ((0, 8),))
    w_in = normal_values(splits[4], (D, 2 * FF), D ** -0.5, 0.21875, ((0, 8),))
    w_mlp_out = normal_values(splits[5], (FF, D), FF ** -0.5, 0.1875, ((1, 8),))
    gain_attn = jnp.clip(1.0 + 0.1 * jax.random.normal(splits[6], (D,), jnp.float32), 0.5, 1.5).astype(jnp.bfloat16)
    gain_mlp = jnp.clip(1.0 + 0.1 * jax.random.normal(splits[7], (D,), jnp.float32), 0.5, 1.5).astype(jnp.bfloat16)
    return {"tokens": tokens, "cotangent": cotangent, "w_qkv": w_qkv, "w_attn_out": w_attn_out, "w_in": w_in, "w_mlp_out": w_mlp_out, "gain_attn": gain_attn, "gain_mlp": gain_mlp}


PRECISE = lax.Precision.HIGHEST
EPSILON = 1e-05
MASKED = -1e+30

@jax.custom_vjp
def low(v):
    return lax.optimization_barrier(v.astype(jnp.bfloat16)).astype(jnp.float32)

@jax.custom_vjp
def low_back(v):
    return v

def low_keep(v):
    return (low(v), None)

def low_pass(kept, grad):
    return (grad,)

def back_keep(v):
    return (v, None)

def back_low(kept, grad):
    return (low(grad),)
low.defvjp(low_keep, low_pass)
low_back.defvjp(back_keep, back_low)

def normalize(field, norm_gain):
    centered = field - lax.optimization_barrier(jnp.mean(field, axis=-1, keepdims=True))
    inverse = lax.rsqrt(lax.optimization_barrier(jnp.mean(centered * centered, axis=-1, keepdims=True)) + EPSILON)
    return centered * inverse * norm_gain

def rope_tables(positions, head_dim):
    half_dim = head_dim // 2
    frequency = 10000.0 ** (-(2.0 * jnp.arange(half_dim, dtype=jnp.float32)) / head_dim)
    angles = positions.astype(jnp.float32)[:, None] * frequency[None, :]
    cosine_table = jnp.concatenate([jnp.cos(angles), jnp.cos(angles)], axis=1)
    sine_table = jnp.concatenate([jnp.sin(angles), jnp.sin(angles)], axis=1)
    return (cosine_table, sine_table)

def rotate(heads_in, cosine_table, sine_table):
    half_dim = heads_in.shape[-1] // 2
    turned = jnp.concatenate([-heads_in[..., half_dim:], heads_in[..., :half_dim]], axis=-1)
    return heads_in * cosine_table[:, None, :] + turned * sine_table[:, None, :]

def attend(queries, key_heads, value_heads):
    length = queries.shape[0]
    block_rows = math.gcd(length, 512)
    padded_keys = jnp.pad(key_heads, ((HALF, HALF), (0, 0), (0, 0)))
    padded_values = jnp.pad(value_heads, ((HALF, HALF), (0, 0), (0, 0)))
    score_scale = queries.shape[-1] ** (-0.5)

    def one_block(block_index):
        first_row = (block_index * block_rows).astype(jnp.int32)
        query_rows = lax.dynamic_slice_in_dim(queries, first_row, block_rows, 0)
        key_rows = lax.dynamic_slice_in_dim(padded_keys, first_row, block_rows + 2 * HALF, 0)
        value_rows = lax.dynamic_slice_in_dim(padded_values, first_row, block_rows + 2 * HALF, 0)
        scores = low_back(score_scale * jnp.einsum('qhd,khd->hqk', query_rows, key_rows, precision=PRECISE))
        query_pos = first_row + jnp.arange(block_rows, dtype=jnp.int32)
        key_pos = first_row - HALF + jnp.arange(block_rows + 2 * HALF, dtype=jnp.int32)
        allowed = (key_pos[None, :] >= 0) & (key_pos[None, :] < length) & (jnp.abs(query_pos[:, None] - key_pos[None, :]) <= HALF)
        scores = jnp.where(allowed[None], scores, MASKED)
        row_max = lax.optimization_barrier(jnp.max(scores, axis=-1, keepdims=True))
        exponents = jnp.exp(scores - row_max)
        attn_weights = low(exponents / lax.optimization_barrier(jnp.sum(exponents, axis=-1, keepdims=True)))
        return jnp.einsum('hqk,khd->qhd', attn_weights, value_rows, precision=PRECISE)
    blocks = lax.map(jax.checkpoint(one_block), jnp.arange(length // block_rows, dtype=jnp.int32))
    return blocks.reshape(queries.shape)

def forward(inputs, w_qkv, w_attn_out, w_in, w_mlp_out, gain_attn, gain_mlp):
    length = inputs.shape[0]
    width = inputs.shape[1]
    head_dim = width // HEADS
    first_in = low(normalize(inputs, gain_attn))
    mixed_qkv = low_back(jnp.dot(first_in, w_qkv, precision=PRECISE))
    cosine_table, sine_table = rope_tables(jnp.arange(length, dtype=jnp.int32), head_dim)
    queries = low(rotate(mixed_qkv[:, :width].reshape(length, HEADS, head_dim), cosine_table, sine_table))
    key_heads = low(rotate(mixed_qkv[:, width:2 * width].reshape(length, HEADS, head_dim), cosine_table, sine_table))
    value_heads = low(mixed_qkv[:, 2 * width:].reshape(length, HEADS, head_dim))
    attended = low(low_back(attend(queries, key_heads, value_heads).reshape(length, width)))
    middle = inputs + low_back(jnp.dot(attended, w_attn_out, precision=PRECISE))
    second_in = low(normalize(middle, gain_mlp))
    gate_up = low_back(jnp.dot(second_in, w_in, precision=PRECISE))
    hidden_units = w_mlp_out.shape[0]
    product = low(jax.nn.gelu(gate_up[:, :hidden_units], approximate=True) * gate_up[:, hidden_units:])
    return middle + jnp.dot(product, w_mlp_out, precision=PRECISE)

def reference(tokens, cotangent, w_qkv, w_attn_out, w_in, w_mlp_out, gain_attn, gain_mlp):
    parameters = tuple((item.astype(jnp.float32) for item in (w_qkv, w_attn_out, w_in, w_mlp_out, gain_attn, gain_mlp)))

    def one_sequence(totals, sequence_pair):
        seq_tokens, seq_grad = sequence_pair
        result, pullback = jax.vjp(forward, seq_tokens.astype(jnp.float32), *parameters)
        gradients = pullback(seq_grad.astype(jnp.float32))
        new_totals = tuple((total_item + grad_item for total_item, grad_item in zip(totals, gradients[1:])))
        return (new_totals, (result.astype(jnp.bfloat16), gradients[0]))
    zeros_init = tuple((jnp.zeros(item.shape, jnp.float32) for item in parameters))
    sums, (outputs, grad_tokens) = lax.scan(one_sequence, zeros_init, (tokens, cotangent))
    return (outputs, grad_tokens, sums[0], sums[1], sums[2], sums[3], sums[4], sums[5])
```

```python
import functools

import jax
import jax.numpy as jnp
from jax import lax
from jax.experimental import pallas as pl
from jax.experimental.pallas import tpu as pltpu
from jax.sharding import PartitionSpec as P

HEADS = 12
HALF = 64
EPSILON = 1e-05
MASKED = -1e30
F32 = jnp.float32
BF16 = jnp.bfloat16


def dot(a, b, dims=((1,), (0,))):
    return lax.dot_general(a, b, (dims, ((), ())), preferred_element_type=F32)


def send_core(value):
    count = lax.axis_size("fsdp")
    return lax.ppermute(value, "fsdp", [(i, i ^ 1) for i in range(count)])


def send_z(value, step):
    count = lax.axis_size("fsdp")
    return lax.ppermute(value, "fsdp", [(i, i ^ (2 * step)) for i in range(count)])


def send_seq(value, step):
    count = lax.axis_size("seq")
    return lax.ppermute(value, "seq", [(i, i ^ step) for i in range(count)])


def send_along(value, step):
    count = lax.axis_size("seq")
    first, last = (max(0, -step), min(count, count - step))
    return lax.ppermute(value, "seq", [(i, i + step) for i in range(first, last)])


def gather_pieces(shard, mine):
    planes = lax.axis_size("fsdp") // 2
    blocks = lax.axis_size("seq")
    along = jnp.stack([send_z(mine, k) for k in range(1, planes)])
    across = [send_seq(along, j) for j in range(1, blocks)]
    own = [shard, along] + across
    return own, [send_core(piece) for piece in own]


def assemble_kernel(widths, planes, blocks, *refs):
    count = 1 + blocks
    sources = (refs[:count], refs[count : 2 * count])
    outs = refs[2 * count :]
    me = lax.axis_index("fsdp")
    here = lax.axis_index("seq")
    plane, core = me // 2, me % 2

    def put(source, index, to):
        start = 0
        for out, width in zip(outs, widths):
            out[to] = source[index, :, start : start + width]
            start += width

    for side in range(2):
        parity = core ^ side
        for j in range(blocks):
            put(sources[side][0], j, (plane * 2 + parity) * blocks + j)
            for k in range(1, planes):
                to = ((plane ^ k) * 2 + parity) * blocks + (here ^ j)
                put(sources[side][1 + j], k - 1, to)


def assemble(own, other, widths):
    planes = lax.axis_size("fsdp") // 2
    blocks = lax.axis_size("seq")
    n = own[0].shape[1]
    total = planes * 2 * blocks
    outs = pl.pallas_call(
        functools.partial(assemble_kernel, widths, planes, blocks),
        out_shape=[jax.ShapeDtypeStruct((total, n, w), BF16) for w in widths],
        in_specs=[pl.BlockSpec(memory_space=pltpu.VMEM)] * (2 * (1 + blocks)),
        out_specs=[pl.BlockSpec(memory_space=pltpu.VMEM)] * len(widths),
        compiler_params=pltpu.CompilerParams(vmem_limit_bytes=48 * 2**20),
        name="assemble",
    )(*own, *other)
    return [out.reshape(total * n, w) for out, w in zip(outs, widths)]


def grads_kernel(blocks, *refs):
    outs = refs[4:]
    own_a, other_a, own_b, other_b = (ref[...] for ref in refs[:4])
    rows = own_a.shape[0] // blocks
    for j in range(blocks):
        part = slice(j * rows, (j + 1) * rows)
        outs[j][...] = (dot(own_a[part], own_b) + dot(other_a[part], other_b)).astype(BF16)


def partial_grads(own_a, other_a, own_b, other_b, widths):
    blocks = lax.axis_size("seq")
    count, depth, tokens = own_a.shape
    total = sum(widths)
    tile = 384
    rows = depth // blocks
    ends = [sum(widths[: x + 1]) // tile for x in range(count - 1)]

    def which(i):
        return sum([(i >= end).astype(jnp.int32) for end in ends], jnp.int32(0))

    a_spec = pl.BlockSpec((None, depth, tokens), lambda i: (which(i), 0, 0))
    b_spec = pl.BlockSpec((tokens, tile), lambda i: (0, i))
    return pl.pallas_call(
        functools.partial(grads_kernel, blocks),
        grid=(total // tile,),
        out_shape=[jax.ShapeDtypeStruct((rows, total), BF16)] * blocks,
        in_specs=[a_spec, a_spec, b_spec, b_spec],
        out_specs=[pl.BlockSpec((rows, tile), lambda i: (0, i))] * blocks,
        name="weight_grads",
    )(own_a, other_a, own_b, other_b)


def reduce_grads(parts):
    planes = lax.axis_size("fsdp") // 2
    blocks = lax.axis_size("seq")
    width = parts[0].shape[1]
    parts = [part.reshape(planes, -1, width) for part in parts]
    arrived = [parts[0]] + [send_seq(parts[j], j) for j in range(1, blocks)]
    sums = [
        functools.reduce(jnp.add, [piece[k].astype(F32) for piece in arrived]).astype(BF16)
        for k in range(planes)
    ]
    landed = [sums[0]] + [send_z(sums[k], k) for k in range(1, planes)]
    mine = functools.reduce(jnp.add, [piece.astype(F32) for piece in landed]).astype(BF16)
    pieces = [mine] + [send_seq(mine, j) for j in range(1, blocks)]
    here = lax.axis_index("seq")
    rows = []
    for i in range(blocks):
        row = pieces[0]
        for j in range(1, blocks):
            row = jnp.where((here ^ j) == i, pieces[j], row)
        rows.append(row)
    return jnp.concatenate(rows, axis=0).astype(F32)


def row_order(width):
    planes = lax.axis_size("fsdp") // 2
    blocks = lax.axis_size("seq")
    n = width // (planes * 2 * blocks)
    me = lax.axis_index("fsdp")
    r = lax.broadcasted_iota(jnp.int32, (width, 1), 0)
    i = r % n
    k = (r // n) % planes
    j = (r // (n * planes)) % blocks
    c = r // (n * planes * blocks)
    f = (((me // 2) ^ k) * 2) + ((me % 2) ^ c)
    natural = (f * blocks + (lax.axis_index("seq") ^ j)) * n + i
    d = lax.broadcasted_iota(jnp.int32, (width, width), 1)
    return (d == natural).astype(BF16)


def normalized(field):
    centered = field - jnp.mean(field, axis=-1, keepdims=True)
    inverse = lax.rsqrt(jnp.mean(centered * centered, axis=-1, keepdims=True) + EPSILON)
    return centered * inverse, inverse


def norm_back(grad_normal, normal, inverse):
    return inverse * (
        grad_normal
        - jnp.mean(grad_normal, axis=-1, keepdims=True)
        - normal * jnp.mean(grad_normal * normal, axis=-1, keepdims=True)
    )


def rope_tables(positions, head_dim):
    half_dim = head_dim // 2
    frequency = 10000.0 ** (-(2.0 * jnp.arange(half_dim, dtype=F32)) / head_dim)
    angles = positions.astype(F32)[:, None] * frequency[None, :]
    cosine_table = jnp.concatenate([jnp.cos(angles), jnp.cos(angles)], axis=1)
    sine_table = jnp.concatenate([jnp.sin(angles), jnp.sin(angles)], axis=1)
    return (cosine_table, sine_table)


def rotate(heads_in, cosine_table, sine_table):
    half_dim = heads_in.shape[-1] // 2
    turned = jnp.concatenate([-heads_in[..., half_dim:], heads_in[..., :half_dim]], axis=-1)
    return heads_in * cosine_table[:, None, :] + turned * sine_table[:, None, :]


def unrotate(grad_heads, cosine_table, sine_table):
    half_dim = grad_heads.shape[-1] // 2
    scaled = grad_heads * sine_table[:, None, :]
    turned_back = jnp.concatenate([scaled[..., half_dim:], -scaled[..., :half_dim]], axis=-1)
    return grad_heads * cosine_table[:, None, :] + turned_back


def gelu_tanh(field):
    return jax.nn.gelu(field, approximate=True)


def on_device(tokens, cotangent, w_qkv, w_attn_out, w_in, w_mlp_out, gain_attn, gain_mlp):
    row_count = tokens.shape[1]
    width = tokens.shape[2]
    head_dim = width // HEADS
    hidden = w_mlp_out.shape[0]
    score_scale = head_dim ** (-0.5)
    blocks = lax.axis_size("seq")
    here = lax.axis_index("seq")
    n = w_qkv.shape[0] // blocks

    gain_one = gain_attn.astype(F32)[:, None]
    gain_two = gain_mlp.astype(F32)[:, None]
    shard_qkv = (w_qkv.astype(F32) * gain_one).astype(BF16).reshape(blocks, n, -1)
    mine_qkv = lax.dynamic_index_in_dim(shard_qkv, here, 0, keepdims=False)
    own, other = gather_pieces(shard_qkv, mine_qkv)

    inputs_low = tokens[0]
    before = send_along(inputs_low[row_count - HALF :], 1)
    after = send_along(inputs_low[:HALF], -1)
    wide = jnp.concatenate([before, inputs_low, after], axis=0).astype(F32)

    rest = jnp.concatenate(
        [w_attn_out, (w_in.astype(F32) * gain_two).astype(BF16), w_mlp_out.T], axis=1
    ).reshape(blocks, n, -1)
    mine_rest = lax.dynamic_index_in_dim(rest, here, 0, keepdims=False)
    own_rest, other_rest = gather_pieces(rest, mine_rest)

    (full_qkv,) = assemble(own, other, (3 * width,))
    full_attn_out, full_in, full_mlp = assemble(
        own_rest, other_rest, (width, 2 * hidden, hidden)
    )
    order = row_order(width)

    first_row = here * row_count
    length = row_count * blocks
    key_pos = first_row - HALF + jnp.arange(row_count + 2 * HALF, dtype=jnp.int32)
    positions = key_pos[HALF : HALF + row_count]
    cosine_wide, sine_wide = rope_tables(key_pos, head_dim)
    cosine_table = cosine_wide[HALF : HALF + row_count]
    sine_table = sine_wide[HALF : HALF + row_count]
    allowed = (
        (key_pos[None, :] >= 0)
        & (key_pos[None, :] < length)
        & (jnp.abs(positions[:, None] - key_pos[None, :]) <= HALF)
    )
    inputs = inputs_low.astype(F32)
    normal_wide, inverse_wide = normalized(wide)
    first_wide = normal_wide.astype(BF16)
    normal_one = normal_wide[HALF : HALF + row_count]
    inverse_one = inverse_wide[HALF : HALF + row_count]
    first_in = first_wide[HALF : HALF + row_count]
    mixed_q = dot(first_in, full_qkv[:, :width])
    mixed_kv = dot(first_wide, full_qkv[:, width:])
    queries = rotate(
        mixed_q.reshape(row_count, HEADS, head_dim), cosine_table, sine_table
    ).astype(BF16)
    key_heads = rotate(
        mixed_kv[:, :width].reshape(-1, HEADS, head_dim), cosine_wide, sine_wide
    ).astype(BF16)
    value_heads = mixed_kv[:, width:].astype(BF16).reshape(-1, HEADS, head_dim)

    scores = (
        jnp.einsum("qhd,khd->hqk", queries, key_heads, preferred_element_type=F32) * score_scale
    )
    scores = jnp.where(allowed[None], scores, MASKED)
    row_max = jnp.max(scores, axis=-1, keepdims=True)
    exponents = jnp.exp(scores - row_max)
    row_sum = jnp.sum(exponents, axis=-1, keepdims=True)
    attn_weights = exponents / row_sum
    attn_low = attn_weights.astype(BF16)
    attended = (
        jnp.einsum("hqk,khd->qhd", attn_low, value_heads, preferred_element_type=F32)
        .reshape(row_count, width)
        .astype(BF16)
    )
    middle = inputs + dot(attended, full_attn_out)
    normal_two, inverse_two = normalized(middle)
    second_in = normal_two.astype(BF16)
    gate_up = dot(second_in, full_in)
    gate_part = gate_up[:, :hidden]
    up_part = gate_up[:, hidden:]
    activated, gelu_pull = jax.vjp(gelu_tanh, gate_part)
    product_low = (activated * up_part).astype(BF16)
    outputs = middle + dot(product_low, full_mlp, ((1,), (1,)))

    def ordered(field):
        moved = dot(order, field, ((1,), (1,))).astype(BF16)
        return moved[: width // 2], moved[width // 2 :]

    def shared_grads(lefts, rights):
        moved = [ordered(left) for left in lefts]
        own_a = jnp.stack([m[0] for m in moved])
        sent_a = jnp.stack([m[1] for m in moved])
        own_b = jnp.concatenate(rights, axis=1)
        widths = tuple(right.shape[1] for right in rights)
        return partial_grads(own_a, send_core(sent_a), own_b, send_core(own_b), widths)

    grad_out = cotangent[0]
    grad_product = dot(grad_out, full_mlp)
    grad_gate = gelu_pull(grad_product * up_part)[0]
    grad_gate_up = jnp.concatenate([grad_gate, grad_product * activated], axis=1).astype(BF16)
    grad_normal_two = dot(grad_gate_up, full_in, ((1,), (1,)))
    grad_middle = grad_out.astype(F32) + norm_back(grad_normal_two, normal_two, inverse_two)
    grad_attn_low = grad_middle.astype(BF16)
    parts_rest = shared_grads(
        (attended, second_in, grad_out), (grad_attn_low, grad_gate_up, product_low)
    )
    grad_attended = (
        dot(grad_attn_low, full_attn_out, ((1,), (1,)))
        .astype(BF16)
        .reshape(row_count, HEADS, head_dim)
    )
    grad_values = jnp.einsum("hqk,qhd->khd", attn_low, grad_attended, preferred_element_type=F32)
    grad_probs = jnp.einsum(
        "qhd,khd->hqk", grad_attended, value_heads, preferred_element_type=F32
    )
    grad_scores = attn_weights * (
        grad_probs - jnp.sum(attn_weights * grad_probs, axis=-1, keepdims=True)
    )
    grad_scores_low = grad_scores.astype(BF16)
    grad_queries = (
        jnp.einsum("hqk,khd->qhd", grad_scores_low, key_heads, preferred_element_type=F32)
        * score_scale
    )
    grad_keys = (
        jnp.einsum("hqk,qhd->khd", grad_scores_low, queries, preferred_element_type=F32)
        * score_scale
    )
    grad_edges = jnp.concatenate(
        [grad_keys.reshape(-1, width), grad_values.reshape(-1, width)], axis=1
    )
    from_above = send_along(grad_edges[:HALF].astype(BF16), -1).astype(F32)
    from_below = send_along(grad_edges[row_count + HALF :].astype(BF16), 1).astype(F32)
    grad_kv = grad_edges[HALF : HALF + row_count]
    grad_kv = (
        grad_kv
        + jnp.pad(from_below, ((0, row_count - HALF), (0, 0)))
        + jnp.pad(from_above, ((row_count - HALF, 0), (0, 0)))
    )
    grad_keys_own = unrotate(
        grad_kv[:, :width].reshape(row_count, HEADS, head_dim), cosine_table, sine_table
    ).reshape(row_count, width)
    grad_query_rows = unrotate(grad_queries, cosine_table, sine_table).reshape(row_count, width)
    grad_mixed = jnp.concatenate(
        [grad_query_rows, grad_keys_own, grad_kv[:, width:]], axis=1
    ).astype(BF16)
    parts_qkv = shared_grads((first_in,), (grad_mixed,))
    grad_normal_one = dot(grad_mixed, full_qkv, ((1,), (1,)))
    grad_inputs = grad_middle + norm_back(grad_normal_one, normal_one, inverse_one)

    sum_rest = reduce_grads(parts_rest)
    sum_attn_out = sum_rest[:, :width]
    sum_in = sum_rest[:, width : width + 2 * hidden]
    sum_mlp = sum_rest[:, width + 2 * hidden :]
    sum_qkv = reduce_grads(parts_qkv)
    return (
        outputs.astype(BF16)[None],
        grad_inputs[None],
        sum_qkv * gain_one,
        sum_attn_out,
        sum_in * gain_two,
        sum_mlp.T,
        jnp.sum(sum_qkv * w_qkv.astype(F32), axis=1),
        jnp.sum(sum_in * w_in.astype(F32), axis=1),
    )


def solution(mesh):
    in_specs = (
        P("fsdp", "seq", None),
        P("fsdp", "seq", None),
        P("fsdp", None),
        P("fsdp", None),
        P("fsdp", None),
        P(None, "fsdp"),
        P("fsdp"),
        P("fsdp"),
    )
    out_specs = (
        P("fsdp", "seq", None),
        P("fsdp", "seq", None),
        P("fsdp", None),
        P("fsdp", None),
        P("fsdp", None),
        P(None, "fsdp"),
        P("fsdp"),
        P("fsdp"),
    )
    return jax.shard_map(
        on_device, mesh=mesh, in_specs=in_specs, out_specs=out_specs, check_vma=False
    )
```

```python
import functools

import jax
import jax.numpy as jnp
from jax import lax
from jax.experimental import pallas as pl
from jax.experimental.pallas import tpu as pltpu
from jax.sharding import PartitionSpec as P

HEADS = 12
HALF = 64
EPSILON = 1e-05
MASKED = -1e30
F32 = jnp.float32
BF16 = jnp.bfloat16


def dot(a, b, dims=((1,), (0,))):
    return lax.dot_general(a, b, (dims, ((), ())), preferred_element_type=F32)


def send_core(value):
    count = lax.axis_size("fsdp")
    return lax.ppermute(value, "fsdp", [(i, i ^ 1) for i in range(count)])


def send_z(value, step):
    count = lax.axis_size("fsdp")
    return lax.ppermute(value, "fsdp", [(i, i ^ (2 * step)) for i in range(count)])


def send_seq(value, step):
    count = lax.axis_size("seq")
    return lax.ppermute(value, "seq", [(i, i ^ step) for i in range(count)])


def send_along(value, step):
    count = lax.axis_size("seq")
    first, last = (max(0, -step), min(count, count - step))
    return lax.ppermute(value, "seq", [(i, i + step) for i in range(first, last)])


def bits_of(count):
    return count.bit_length() - 1


def column_cuts(width):
    parts = bits_of(lax.axis_size("seq"))
    tiles = width // 128
    edges = [(2 * r * tiles + parts) // (2 * parts) * 128 for r in range(parts)] + [width]
    return list(zip(edges[:-1], edges[1:]))


def direction(part, step):
    return 1 << ((part + step) % bits_of(lax.axis_size("seq")))


def along_z(mine, late):
    planes = lax.axis_size("fsdp") // 2
    return [send_z(mine if k < 3 else late, k) for k in range(1, planes)]


def by_range(along):
    return [
        jnp.stack([piece[:, first:last] for piece in along])
        for first, last in column_cuts(along[0].shape[1])
    ]


def across_plane(held, step):
    return [send_seq(value, direction(r, step)) for r, value in enumerate(held)]


def joined_ranges(held, got):
    return [jnp.concatenate(pair) for pair in zip(held, got)]


def across_rest_of_plane(held, got):
    for step in range(1, bits_of(lax.axis_size("seq"))):
        held = joined_ranges(held, got)
        got = across_plane(held, step)
    return held + got


def distances(part):
    found = [0]
    for step in range(bits_of(lax.axis_size("seq"))):
        found = found + [j ^ direction(part, step) for j in found]
    return found


def fits(n):
    return n % 8 == 0


def with_other_core(pieces):
    pieces = pieces + [send_core(piece) for piece in pieces]
    if fits(pieces[0].shape[1]):
        return pieces
    whole = sum(piece.size for piece in pieces)
    blocks, n, width = pieces[0].shape
    out = jnp.zeros((whole // (n * width), n, width), BF16)
    for to, first, last, source, index in placements(pieces, n, width):
        block = lax.dynamic_slice_in_dim(source, index, 1, 0)
        out = lax.dynamic_update_slice(out, block, (to, 0, first))
    return [out.reshape(-1, width)]


def placements(pieces, n, width):
    planes = lax.axis_size("fsdp") // 2
    blocks = lax.axis_size("seq")
    me, here = lax.axis_index("fsdp"), lax.axis_index("seq")
    plane, core = me // 2, me % 2
    half = len(pieces) // 2
    cuts = column_cuts(width)
    found = []
    for side in range(2):
        parity = core ^ side
        own, *others = pieces[side * half : (side + 1) * half]
        for j in range(blocks):
            found.append(((plane * 2 + parity) * blocks + j, 0, width, own, j))
        for r, (first, last) in enumerate(cuts):
            reach = distances(r)
            for m, j in enumerate(reach):
                late = m >= blocks // 2
                source = others[r + late * len(cuts)]
                for k in range(1, planes):
                    to = ((plane ^ k) * 2 + parity) * blocks + (here ^ j)
                    index = (m % (blocks // 2)) * (planes - 1) + k - 1
                    found.append((to, first, last, source, index))
    return found


def weight_scratch(pieces):
    if len(pieces) == 1:
        return []
    blocks, n, width = pieces[0].shape
    return [pltpu.VMEM((lax.axis_size("fsdp") * blocks, n, width), BF16)]


def whole_weight(sources, scratch):
    if not scratch:
        return sources[0][...]
    (out,) = scratch
    _, n, width = out.shape
    for to, first, last, source, index in placements(sources, n, width):
        out[to, :, first:last] = source[index]
    return out[...].reshape(-1, width)


def grads_kernel(widths, own_a, other_a, own_b, other_b, *outs):
    blocks = lax.axis_size("seq")
    cuts = column_cuts(sum(widths))
    start = 0
    for x, width in enumerate(widths):
        left_own, left_other = own_a[x].T, other_a[x].T
        rows = left_own.shape[0] // blocks
        for r, (low, high) in enumerate(cuts):
            keep, sent = outs[2 * r], outs[2 * r + 1]
            for first in range(max(low, start), min(high, start + width), 512):
                last = min(first + 512, high, start + width)
                lanes = slice(first, last)
                total = dot(left_own, own_b[:, lanes]) + dot(left_other, other_b[:, lanes])
                for m, j in enumerate(halving_order(r)):
                    out = sent if m >= blocks // 2 else keep
                    out[m % (blocks // 2), :, first - low : last - low] = total[
                        j * rows : (j + 1) * rows
                    ].astype(BF16)
        start += width


def halving_order(part):
    steps = bits_of(lax.axis_size("seq"))
    return [
        sum(direction(part, t) for t in range(steps) if m >> (steps - 1 - t) & 1)
        for m in range(1 << steps)
    ]


def partial_grads(own_a, other_a, own_b, other_b, widths):
    blocks = lax.axis_size("seq")
    rows = own_a.shape[2] // blocks
    shapes = [
        jax.ShapeDtypeStruct((blocks // 2, rows, last - first), BF16)
        for first, last in column_cuts(sum(widths))
        for _ in range(2)
    ]
    outs = pl.pallas_call(
        functools.partial(grads_kernel, widths),
        out_shape=shapes,
        in_specs=[pl.BlockSpec(memory_space=pltpu.VMEM)] * 4,
        out_specs=[pl.BlockSpec(memory_space=pltpu.VMEM)] * len(shapes),
        compiler_params=pltpu.CompilerParams(vmem_limit_bytes=40 * 2**20),
        name="weight_grads",
    )(own_a, other_a, own_b, other_b)
    return list(outs[::2]), list(outs[1::2])


def halve_kernel(parts, *refs):
    for r in range(parts):
        keep, got = refs[r], refs[parts + r]
        low, high = refs[2 * parts + 2 * r], refs[2 * parts + 2 * r + 1]
        half = low.shape[0]
        low[...] = (keep[:half].astype(F32) + got[:half].astype(F32)).astype(BF16)
        high[...] = (keep[half:].astype(F32) + got[half:].astype(F32)).astype(BF16)


def halve(keep, got):
    parts = len(keep)
    shapes = [
        jax.ShapeDtypeStruct((value.shape[0] // 2,) + value.shape[1:], BF16)
        for value in keep
        for _ in range(2)
    ]
    outs = pl.pallas_call(
        functools.partial(halve_kernel, parts),
        out_shape=shapes,
        in_specs=[pl.BlockSpec(memory_space=pltpu.VMEM)] * (2 * parts),
        out_specs=[pl.BlockSpec(memory_space=pltpu.VMEM)] * (2 * parts),
        compiler_params=pltpu.CompilerParams(vmem_limit_bytes=40 * 2**20),
        name="add_and_halve",
    )(*keep, *got)
    return list(outs[::2]), list(outs[1::2])


def by_plane_kernel(parts, *refs):
    first = 0
    for r in range(parts):
        keep, got = refs[r], refs[parts + r]
        last = first + keep.shape[2]
        for k, out in enumerate(refs[2 * parts :]):
            out[:, first:last] = (keep[k].astype(F32) + got[k].astype(F32)).astype(BF16)
        first = last


def by_plane(keep, got):
    parts = len(keep)
    planes = lax.axis_size("fsdp") // 2
    keep = [value.reshape(planes, -1, value.shape[2]) for value in keep]
    got = [value.reshape(planes, -1, value.shape[2]) for value in got]
    shape = (keep[0].shape[1], sum(value.shape[2] for value in keep))
    return pl.pallas_call(
        functools.partial(by_plane_kernel, parts),
        out_shape=[jax.ShapeDtypeStruct(shape, BF16)] * planes,
        in_specs=[pl.BlockSpec(memory_space=pltpu.VMEM)] * (2 * parts),
        out_specs=[pl.BlockSpec(memory_space=pltpu.VMEM)] * planes,
        compiler_params=pltpu.CompilerParams(vmem_limit_bytes=40 * 2**20),
        name="add_by_plane",
    )(*keep, *got)


def rest_of_plane(keep, got):
    for step in range(1, bits_of(lax.axis_size("seq"))):
        keep, sent = halve(keep, got)
        got = across_plane(sent, step)
    return by_plane(keep, got)


def z_sends(sums):
    return [sums[0]] + [send_z(value, k) for k, value in enumerate(sums) if k > 0]


def spread(landed):
    blocks = lax.axis_size("seq")
    mine = functools.reduce(jnp.add, [piece.astype(F32) for piece in landed]).astype(BF16)
    pieces = [mine] + [send_seq(mine, j) for j in range(1, blocks)]
    here = lax.axis_index("seq")
    rows = []
    for i in range(blocks):
        row = pieces[0]
        for j in range(1, blocks):
            row = jnp.where((here ^ j) == i, pieces[j], row)
        rows.append(row)
    return jnp.concatenate(rows, axis=0).astype(F32)


def row_order(width):
    planes = lax.axis_size("fsdp") // 2
    blocks = lax.axis_size("seq")
    n = width // (planes * 2 * blocks)
    me = lax.axis_index("fsdp")
    r = lax.broadcasted_iota(jnp.int32, (1, width), 1)
    i = r % n
    k = (r // n) % planes
    j = (r // (n * planes)) % blocks
    c = r // (n * planes * blocks)
    f = (((me // 2) ^ k) * 2) + ((me % 2) ^ c)
    natural = (f * blocks + (lax.axis_index("seq") ^ j)) * n + i
    d = lax.broadcasted_iota(jnp.int32, (width, width), 0)
    return (d == natural).astype(BF16)


def normalized(field):
    centered = field - jnp.mean(field, axis=-1, keepdims=True)
    inverse = lax.rsqrt(jnp.mean(centered * centered, axis=-1, keepdims=True) + EPSILON)
    return centered * inverse, inverse


def norm_back(grad_normal, normal, inverse):
    return inverse * (
        grad_normal
        - jnp.mean(grad_normal, axis=-1, keepdims=True)
        - normal * jnp.mean(grad_normal * normal, axis=-1, keepdims=True)
    )


def rope_tables(positions, head_dim):
    half_dim = head_dim // 2
    frequency = 10000.0 ** (-(2.0 * jnp.arange(half_dim, dtype=F32)) / head_dim)
    angles = positions.astype(F32)[:, None] * frequency[None, :]
    cosine, sine = jnp.cos(angles), jnp.sin(angles)
    return (
        jnp.concatenate([cosine] * 4, axis=1),
        jnp.concatenate([-sine, sine, -sine, sine], axis=1),
    )


def turned(pair, head_dim):
    lane = lax.broadcasted_iota(jnp.int32, pair.shape, 1)
    wide = pair.shape[1]
    half_dim = head_dim // 2
    return jnp.where(
        lane % head_dim < half_dim,
        pltpu.roll(pair, wide - half_dim, 1),
        pltpu.roll(pair, half_dim, 1),
    )


def attention_kernel(
    head_dim,
    count,
    before_ref,
    inputs_ref,
    after_ref,
    cosine_ref,
    sine_ref,
    *refs,
):
    first_ref, queries_ref, keys_ref, values_ref, probs_ref, attended_ref = refs[count : count + 6]
    weight = whole_weight(refs[:count], refs[count + 6 :])
    row_count, width = inputs_ref.shape
    wide = row_count + 2 * HALF
    pair = 2 * head_dim
    rows = jnp.concatenate([before_ref[...], inputs_ref[...], after_ref[...]], axis=0)
    normal, _ = normalized(rows.astype(F32))
    first_wide = normal.astype(BF16)
    first_in = first_wide[HALF : HALF + row_count]
    first_ref[...] = first_in
    cosine, sine = cosine_ref[...], sine_ref[...]
    own_cosine, own_sine = (t[HALF : HALF + row_count] for t in (cosine, sine))
    here = lax.axis_index("seq")
    length = row_count * lax.axis_size("seq")
    first_key = here * row_count - HALF
    row = lax.broadcasted_iota(jnp.int32, (row_count, wide), 0)
    column = lax.broadcasted_iota(jnp.int32, (row_count, wide), 1)
    distance = column - HALF - row
    key_pos = first_key + column
    allowed = (key_pos >= 0) & (key_pos < length) & (jnp.abs(distance) <= HALF)
    low_lanes = lax.broadcasted_iota(jnp.int32, (row_count, pair), 1) < head_dim

    mixed_q = dot(first_in, weight[:, :width])
    mixed_k = dot(first_wide, weight[:, width : 2 * width])
    values_ref[...] = dot(first_wide, weight[:, 2 * width :]).astype(BF16)
    for p in range(width // pair):
        lanes = slice(p * pair, (p + 1) * pair)
        q = mixed_q[:, lanes]
        k = mixed_k[:, lanes]
        q = (q * own_cosine + turned(q, head_dim) * own_sine).astype(BF16)
        q = (q.astype(F32) * head_dim**-0.5).astype(BF16)
        k = (k * cosine + turned(k, head_dim) * sine).astype(BF16)
        queries_ref[:, lanes] = q
        keys_ref[:, lanes] = k
        v = values_ref[:, lanes]
        heads = []
        for side in range(2):
            mine = low_lanes if side == 0 else ~low_lanes
            scores = dot(jnp.where(mine, q, jnp.zeros_like(q)), k, ((1,), (1,)))
            scores = jnp.where(allowed, scores, MASKED)
            row_max = jnp.max(scores, axis=-1, keepdims=True)
            exponents = jnp.exp(scores - row_max)
            row_sum = jnp.sum(exponents, axis=-1, keepdims=True)
            weights = (exponents / row_sum).astype(BF16)
            probs_ref[2 * p + side] = weights
            heads.append(dot(weights, v))
        attended_ref[:, lanes] = jnp.where(low_lanes, heads[0], heads[1]).astype(BF16)


def attention_forward(before, inputs, after, cosine, sine, pieces, head_dim):
    row_count, width = inputs.shape
    wide = row_count + 2 * HALF
    heads = width // head_dim
    shapes = (
        (row_count, width),
        (row_count, width),
        (wide, width),
        (wide, width),
        (heads, row_count, wide),
        (row_count, width),
    )
    return pl.pallas_call(
        functools.partial(attention_kernel, head_dim, len(pieces)),
        out_shape=[jax.ShapeDtypeStruct(shape, BF16) for shape in shapes],
        in_specs=[pl.BlockSpec(memory_space=pltpu.VMEM)] * (5 + len(pieces)),
        out_specs=[pl.BlockSpec(memory_space=pltpu.VMEM)] * 6,
        scratch_shapes=weight_scratch(pieces),
        compiler_params=pltpu.CompilerParams(vmem_limit_bytes=40 * 2**20),
        name="attention_forward",
    )(before, inputs, after, cosine, sine, *pieces)


def mlp_kernel(count, inputs_ref, attended_ref, cotangent_ref, order_ref, *refs):
    outputs_ref, grad_middle_ref, grad_attended_ref = refs[count : count + 3]
    right_ref, own_left_ref, sent_left_ref = refs[count + 3 : count + 6]
    weight = whole_weight(refs[:count], refs[count + 6 :])
    width = inputs_ref.shape[1]
    hidden = (weight.shape[1] - width) // 3
    attn_out = slice(0, width)
    into = slice(width, width + 2 * hidden)
    back = slice(width + 2 * hidden, width + 3 * hidden)
    transposed = ((1,), (1,))
    attended = attended_ref[...]
    middle = inputs_ref[...].astype(F32) + dot(attended, weight[:, attn_out])
    normal, inverse = normalized(middle)
    second_in = normal.astype(BF16)
    gate_up = dot(second_in, weight[:, into])
    gate, up = gate_up[:, :hidden], gate_up[:, hidden:]
    slope = (2.0 / jnp.pi) ** 0.5
    square = gate * gate
    level = jnp.tanh(slope * (gate + 0.044715 * gate * square))
    activated = 0.5 * gate * (1.0 + level)
    steep = 0.5 * (1.0 + level) + 0.5 * gate * (1.0 - level * level) * slope * (
        1.0 + 3 * 0.044715 * square
    )
    product = (activated * up).astype(BF16)
    outputs_ref[...] = (middle + dot(product, weight[:, back], transposed)).astype(BF16)
    grad_out = cotangent_ref[...]
    grad_product = dot(grad_out, weight[:, back])
    grad_gate_up = jnp.concatenate(
        [grad_product * up * steep, grad_product * activated], axis=1
    ).astype(BF16)
    grad_normal = dot(grad_gate_up, weight[:, into], transposed)
    grad_middle = grad_out.astype(F32) + norm_back(grad_normal, normal, inverse)
    grad_middle_ref[...] = grad_middle
    grad_attn_low = grad_middle.astype(BF16)
    grad_attended_ref[...] = dot(grad_attn_low, weight[:, attn_out], transposed).astype(BF16)
    right_ref[:, attn_out] = grad_attn_low
    right_ref[:, into] = grad_gate_up
    right_ref[:, back] = product
    depth = width // 2
    for x, left in enumerate((attended, second_in, grad_out)):
        moved = dot(left, order_ref[...]).astype(BF16)
        own_left_ref[x] = moved[:, :depth]
        sent_left_ref[x] = moved[:, depth:]


def mlp_both_ways(inputs, attended, cotangent, order, pieces):
    row_count, width = inputs.shape
    shapes = (
        ((row_count, width), BF16),
        ((row_count, width), F32),
        ((row_count, width), BF16),
        ((row_count, pieces[0].shape[-1]), BF16),
        ((3, row_count, width // 2), BF16),
        ((3, row_count, width // 2), BF16),
    )
    return pl.pallas_call(
        functools.partial(mlp_kernel, len(pieces)),
        out_shape=[jax.ShapeDtypeStruct(*shape) for shape in shapes],
        in_specs=[pl.BlockSpec(memory_space=pltpu.VMEM)] * (4 + len(pieces)),
        out_specs=[pl.BlockSpec(memory_space=pltpu.VMEM)] * 6,
        scratch_shapes=weight_scratch(pieces),
        compiler_params=pltpu.CompilerParams(vmem_limit_bytes=48 * 2**20),
        name="mlp_both_ways",
    )(inputs, attended, cotangent, order, *pieces)


def attention_back_kernel(
    head_dim,
    grad_ref,
    probs_ref,
    queries_ref,
    keys_ref,
    values_ref,
    cosine_ref,
    sine_ref,
    grad_queries_ref,
    own_ref,
    low_ref,
    high_ref,
):
    row_count, width = grad_ref.shape
    pair = 2 * head_dim
    cosine, sine = cosine_ref[...], sine_ref[...]
    own_cosine, own_sine = (t[HALF : HALF + row_count] for t in (cosine, sine))
    low_lanes = lax.broadcasted_iota(jnp.int32, (row_count, pair), 1) < head_dim
    over_rows = ((0,), (0,))

    def put(field, lanes):
        low_ref[:, lanes] = field[:HALF].astype(BF16)
        own_ref[:, lanes] = field[HALF : HALF + row_count]
        high_ref[:, lanes] = field[HALF + row_count :].astype(BF16)

    for p in range(width // pair):
        lanes = slice(p * pair, (p + 1) * pair)
        grad, q = grad_ref[:, lanes], queries_ref[:, lanes]
        k, v = keys_ref[:, lanes], values_ref[:, lanes]
        grad_q, grad_k, grad_v = [], 0.0, 0.0
        for side in range(2):
            mine = low_lanes if side == 0 else ~low_lanes
            weights_low = probs_ref[2 * p + side]
            weights = weights_low.astype(F32)
            grad_mine = jnp.where(mine, grad, jnp.zeros_like(grad))
            q_mine = jnp.where(mine, q, jnp.zeros_like(q))
            grad_probs = dot(grad_mine, v, ((1,), (1,)))
            weighted = weights * grad_probs
            grad_scores = (
                weighted - weights * jnp.sum(weighted, axis=-1, keepdims=True)
            ).astype(BF16)
            grad_q.append(dot(grad_scores, k))
            grad_k = grad_k + dot(grad_scores, q_mine, over_rows)
            grad_v = grad_v + dot(weights_low, grad_mine, over_rows)
        turn = jnp.where(low_lanes, grad_q[0], grad_q[1]) * head_dim**-0.5
        grad_queries_ref[:, lanes] = (
            turn * own_cosine - turned(turn, head_dim) * own_sine
        ).astype(BF16)
        put(grad_k * cosine - turned(grad_k, head_dim) * sine, lanes)
        put(grad_v, slice(width + p * pair, width + (p + 1) * pair))


def attention_backward(grad, probs, queries, keys, values, cosine, sine, head_dim):
    row_count, width = grad.shape
    shapes = (
        ((row_count, width), BF16),
        ((row_count, 2 * width), F32),
        ((HALF, 2 * width), BF16),
        ((HALF, 2 * width), BF16),
    )
    return pl.pallas_call(
        functools.partial(attention_back_kernel, head_dim),
        out_shape=[jax.ShapeDtypeStruct(*shape) for shape in shapes],
        in_specs=[pl.BlockSpec(memory_space=pltpu.VMEM)] * 7,
        out_specs=[pl.BlockSpec(memory_space=pltpu.VMEM)] * 4,
        compiler_params=pltpu.CompilerParams(vmem_limit_bytes=40 * 2**20),
        name="attention_backward",
    )(grad, probs, queries, keys, values, cosine, sine)


def mixed_kernel(grad_queries_ref, own_ref, below_ref, above_ref, out_ref):
    row_count, width = grad_queries_ref.shape
    out_ref[:, :width] = grad_queries_ref[...]
    low, high = own_ref[:HALF], own_ref[row_count - HALF :]
    out_ref[:HALF, width:] = (low + below_ref[...].astype(F32)).astype(BF16)
    out_ref[HALF:, width:] = (high + above_ref[...].astype(F32)).astype(BF16)


def mixed_grads(grad_queries, own, below, above):
    row_count, width = grad_queries.shape
    return pl.pallas_call(
        mixed_kernel,
        out_shape=jax.ShapeDtypeStruct((row_count, 3 * width), BF16),
        in_specs=[pl.BlockSpec(memory_space=pltpu.VMEM)] * 4,
        out_specs=pl.BlockSpec(memory_space=pltpu.VMEM),
        name="mixed_grads",
    )(grad_queries, own, below, above)


def input_grads_kernel(count, mixed_ref, inputs_ref, middle_ref, *refs):
    out_ref = refs[count]
    weight = whole_weight(refs[:count], refs[count + 1 :])
    normal, inverse = normalized(inputs_ref[...].astype(F32))
    grad_normal = dot(mixed_ref[...], weight, ((1,), (1,)))
    out_ref[...] = middle_ref[...] + norm_back(grad_normal, normal, inverse)


def input_grads(mixed, inputs, grad_middle, pieces):
    return pl.pallas_call(
        functools.partial(input_grads_kernel, len(pieces)),
        out_shape=jax.ShapeDtypeStruct(inputs.shape, F32),
        in_specs=[pl.BlockSpec(memory_space=pltpu.VMEM)] * (3 + len(pieces)),
        out_specs=pl.BlockSpec(memory_space=pltpu.VMEM),
        scratch_shapes=weight_scratch(pieces),
        compiler_params=pltpu.CompilerParams(vmem_limit_bytes=40 * 2**20),
        name="input_grads",
    )(mixed, inputs, grad_middle, *pieces)


def on_device(tokens, cotangent, w_qkv, w_attn_out, w_in, w_mlp_out, gain_attn, gain_mlp):
    row_count = tokens.shape[1]
    width = tokens.shape[2]
    head_dim = width // HEADS
    hidden = w_mlp_out.shape[0]
    blocks = lax.axis_size("seq")
    here = lax.axis_index("seq")
    n = w_qkv.shape[0] // blocks

    together = lax.optimization_barrier

    gain_one = gain_attn.astype(F32)[:, None]
    gain_two = gain_mlp.astype(F32)[:, None]

    def quarter(value):
        return lax.dynamic_slice_in_dim(value, here * n, n, 0)

    inputs_low = tokens[0]
    mine = (quarter(w_qkv).astype(F32) * quarter(gain_one)).astype(BF16)
    along = along_z(mine, mine)
    before = send_along(inputs_low[row_count - HALF :], 1)
    after = send_along(inputs_low[:HALF], -1)
    along, before, after = together((along, before, after))
    held = by_range(along)
    got = across_plane(held, 0)
    own = (w_qkv.astype(F32) * gain_one).astype(BF16).reshape(blocks, n, -1)

    rest = jnp.concatenate(
        [w_attn_out, (w_in.astype(F32) * gain_two).astype(BF16), w_mlp_out.T], axis=1
    )
    mine_rest, _ = together((quarter(rest), along))
    late_rest, _ = together((mine_rest, got))
    along_rest = along_z(mine_rest, late_rest)

    qkv_pieces = with_other_core([own] + across_rest_of_plane(held, got))
    held_rest = by_range(along_rest)
    got_rest = across_plane(held_rest, 0)

    order = row_order(width)
    key_pos = here * row_count - HALF + jnp.arange(row_count + 2 * HALF, dtype=jnp.int32)
    cosine, sine = rope_tables(key_pos, head_dim)
    inputs_low, got_rest = together((inputs_low, got_rest))
    first_in, queries, keys, values, probs, attended = attention_forward(
        before, inputs_low, after, cosine, sine, qkv_pieces, head_dim
    )
    rest_pieces = with_other_core(
        [rest.reshape(blocks, n, -1)] + across_rest_of_plane(held_rest, got_rest)
    )
    outputs, grad_middle, grad_attended, right, own_left, sent_left = mlp_both_ways(
        inputs_low, attended, cotangent[0], order, rest_pieces
    )
    other_left, other_right = send_core(sent_left), send_core(right)
    grad_queries, grad_own, grad_low, grad_high = attention_backward(
        grad_attended, probs, queries, keys, values, cosine, sine, head_dim
    )
    above = send_along(grad_low, -1)
    below = send_along(grad_high, 1)
    own_left, grad_low = together((own_left, grad_low))
    keep_rest, sent_rest = partial_grads(
        own_left, other_left, right, other_right, (width, 2 * hidden, hidden)
    )
    sent_rest, above, below = together((sent_rest, above, below))
    got_rest = across_plane(sent_rest, 0)

    grad_mixed = mixed_grads(grad_queries, grad_own, below, above)
    moved = dot(first_in, order).astype(BF16)
    own_first, sent_first = moved[None, :, : width // 2], moved[None, :, width // 2 :]
    keep_qkv, sent_qkv = partial_grads(
        own_first, send_core(sent_first), grad_mixed, send_core(grad_mixed), (3 * width,)
    )
    got_rest, sent_qkv = together((got_rest, sent_qkv))
    got_qkv = across_plane(sent_qkv, 0)
    grad_inputs = input_grads(grad_mixed, inputs_low, grad_middle, qkv_pieces)

    sum_rest = spread(z_sends(rest_of_plane(keep_rest, got_rest)))
    sum_qkv = spread(z_sends(rest_of_plane(keep_qkv, got_qkv)))
    sum_attn_out = sum_rest[:, :width]
    sum_in = sum_rest[:, width : width + 2 * hidden]
    sum_mlp = sum_rest[:, width + 2 * hidden :]
    return (
        outputs[None],
        grad_inputs[None],
        sum_qkv * gain_one,
        sum_attn_out,
        sum_in * gain_two,
        sum_mlp.T,
        jnp.sum(sum_qkv * w_qkv.astype(F32), axis=1),
        jnp.sum(sum_in * w_in.astype(F32), axis=1),
    )


def solution(mesh):
    in_specs = (
        P("fsdp", "seq", None),
        P("fsdp", "seq", None),
        P("fsdp", None),
        P("fsdp", None),
        P("fsdp", None),
        P(None, "fsdp"),
        P("fsdp"),
        P("fsdp"),
    )
    out_specs = (
        P("fsdp", "seq", None),
        P("fsdp", "seq", None),
        P("fsdp", None),
        P("fsdp", None),
        P("fsdp", None),
        P(None, "fsdp"),
        P("fsdp"),
        P("fsdp"),
    )
    return jax.shard_map(
        on_device, mesh=mesh, in_specs=in_specs, out_specs=out_specs, check_vma=False
    )
```

```python
import functools

import jax
import jax.numpy as jnp
from jax import lax
from jax.experimental import pallas as pl
from jax.experimental.pallas import tpu as pltpu
from jax.sharding import PartitionSpec as P

HEADS = 12
HALF = 64
EPSILON = 1e-05
MASKED = -1e30
F32 = jnp.float32
BF16 = jnp.bfloat16


def dot(a, b, dims=((1,), (0,))):
    return lax.dot_general(a, b, (dims, ((), ())), preferred_element_type=F32)


def send_core(value):
    count = lax.axis_size("fsdp")
    return lax.ppermute(value, "fsdp", [(i, i ^ 1) for i in range(count)])


def send_z(value, step):
    count = lax.axis_size("fsdp")
    return lax.ppermute(value, "fsdp", [(i, i ^ (2 * step)) for i in range(count)])


def send_seq(value, step):
    count = lax.axis_size("seq")
    return lax.ppermute(value, "seq", [(i, i ^ step) for i in range(count)])


def send_along(value, step):
    count = lax.axis_size("seq")
    first, last = (max(0, -step), min(count, count - step))
    return lax.ppermute(value, "seq", [(i, i + step) for i in range(first, last)])


def bits_of(count):
    return count.bit_length() - 1


def column_cuts(width):
    parts = bits_of(lax.axis_size("seq"))
    tiles = width // 128
    edges = [(2 * r * tiles + parts) // (2 * parts) * 128 for r in range(parts)] + [width]
    return list(zip(edges[:-1], edges[1:]))


def direction(part, step):
    return 1 << ((part + step) % bits_of(lax.axis_size("seq")))


def along_z(mine):
    planes = lax.axis_size("fsdp") // 2
    return [send_z(mine, k) for k in range(1, planes)]


def by_range(along):
    return [
        jnp.stack([piece[:, first:last] for piece in along])
        for first, last in column_cuts(along[0].shape[1])
    ]


def across_plane(held, step):
    return [send_seq(value, direction(r, step)) for r, value in enumerate(held)]


def joined_ranges(held, got):
    return [jnp.concatenate(pair) for pair in zip(held, got)]


def across_rest_of_plane(held, got):
    for step in range(1, bits_of(lax.axis_size("seq"))):
        held = joined_ranges(held, got)
        got = across_plane(held, step)
    return held + got


def distances(part):
    found = [0]
    for step in range(bits_of(lax.axis_size("seq"))):
        found = found + [j ^ direction(part, step) for j in found]
    return found


def fits(n):
    return n % 8 == 0


def with_other_core(pieces):
    pieces = pieces + [send_core(piece) for piece in pieces]
    if fits(pieces[0].shape[1]):
        return pieces
    whole = sum(piece.size for piece in pieces)
    blocks, n, width = pieces[0].shape
    out = jnp.zeros((whole // (n * width), n, width), BF16)
    for to, first, last, source, index in placements(pieces, n, width):
        block = lax.dynamic_slice_in_dim(source, index, 1, 0)
        out = lax.dynamic_update_slice(out, block, (to, 0, first))
    return [out.reshape(-1, width)]


def placements(pieces, n, width):
    planes = lax.axis_size("fsdp") // 2
    blocks = lax.axis_size("seq")
    me, here = lax.axis_index("fsdp"), lax.axis_index("seq")
    plane, core = me // 2, me % 2
    half = len(pieces) // 2
    cuts = column_cuts(width)
    found = []
    for side in range(2):
        parity = core ^ side
        own, *others = pieces[side * half : (side + 1) * half]
        for j in range(blocks):
            found.append(((plane * 2 + parity) * blocks + j, 0, width, own, j))
        for r, (first, last) in enumerate(cuts):
            reach = distances(r)
            for m, j in enumerate(reach):
                late = m >= blocks // 2
                source = others[r + late * len(cuts)]
                for k in range(1, planes):
                    to = ((plane ^ k) * 2 + parity) * blocks + (here ^ j)
                    index = (m % (blocks // 2)) * (planes - 1) + k - 1
                    found.append((to, first, last, source, index))
    return found


def weight_scratch(pieces):
    if len(pieces) == 1:
        return []
    blocks, n, width = pieces[0].shape
    return [pltpu.VMEM((lax.axis_size("fsdp") * blocks, n, width), BF16)]


def whole_weight(sources, scratch):
    if not scratch:
        return sources[0][...]
    (out,) = scratch
    _, n, width = out.shape
    for to, first, last, source, index in placements(sources, n, width):
        out[to, :, first:last] = source[index]
    return out[...].reshape(-1, width)


def grads_kernel(counts, products, *refs):
    lefts, rights = counts
    own_a, other_a = refs[:lefts], refs[lefts : 2 * lefts]
    refs = refs[2 * lefts :]
    own_b, other_b = refs[:rights], refs[rights : 2 * rights]
    outs = refs[2 * rights :]
    blocks = lax.axis_size("seq")
    cuts = column_cuts(sum(product[-1] for product in products))
    start = 0
    for left, index, row, count, right, column, width in products:
        reach = slice(row, row + count)
        left_own, left_other = own_a[left][index, reach].T, other_a[left][index, reach].T
        rows = left_own.shape[0] // blocks
        for r, (low, high) in enumerate(cuts):
            keep, sent = outs[2 * r], outs[2 * r + 1]
            for first in range(max(low, start), min(high, start + width), 512):
                last = min(first + 512, high, start + width)
                lanes = slice(column + first - start, column + last - start)
                total = dot(left_own, own_b[right][:, lanes]) + dot(
                    left_other, other_b[right][:, lanes]
                )
                for m, j in enumerate(halving_order(r)):
                    out = sent if m >= blocks // 2 else keep
                    out[m % (blocks // 2), :, first - low : last - low] = total[
                        j * rows : (j + 1) * rows
                    ].astype(BF16)
        start += width


def halving_order(part):
    steps = bits_of(lax.axis_size("seq"))
    return [
        sum(direction(part, t) for t in range(steps) if m >> (steps - 1 - t) & 1)
        for m in range(1 << steps)
    ]


def partial_grads(own_a, other_a, own_b, other_b, products):
    blocks = lax.axis_size("seq")
    rows = own_a[0].shape[2] // blocks
    shapes = [
        jax.ShapeDtypeStruct((blocks // 2, rows, last - first), BF16)
        for first, last in column_cuts(sum(product[-1] for product in products))
        for _ in range(2)
    ]
    operands = [*own_a, *other_a, *own_b, *other_b]
    outs = pl.pallas_call(
        functools.partial(grads_kernel, (len(own_a), len(own_b)), products),
        out_shape=shapes,
        in_specs=[pl.BlockSpec(memory_space=pltpu.VMEM)] * len(operands),
        out_specs=[pl.BlockSpec(memory_space=pltpu.VMEM)] * len(shapes),
        compiler_params=pltpu.CompilerParams(vmem_limit_bytes=40 * 2**20),
        name="weight_grads",
    )(*operands)
    return list(outs[::2]), list(outs[1::2])


def halve_kernel(parts, *refs):
    for r in range(parts):
        keep, got = refs[r], refs[parts + r]
        low, high = refs[2 * parts + 2 * r], refs[2 * parts + 2 * r + 1]
        half = low.shape[0]
        low[...] = (keep[:half].astype(F32) + got[:half].astype(F32)).astype(BF16)
        high[...] = (keep[half:].astype(F32) + got[half:].astype(F32)).astype(BF16)


def halve(keep, got):
    parts = len(keep)
    shapes = [
        jax.ShapeDtypeStruct((value.shape[0] // 2,) + value.shape[1:], BF16)
        for value in keep
        for _ in range(2)
    ]
    outs = pl.pallas_call(
        functools.partial(halve_kernel, parts),
        out_shape=shapes,
        in_specs=[pl.BlockSpec(memory_space=pltpu.VMEM)] * (2 * parts),
        out_specs=[pl.BlockSpec(memory_space=pltpu.VMEM)] * (2 * parts),
        compiler_params=pltpu.CompilerParams(vmem_limit_bytes=40 * 2**20),
        name="add_and_halve",
    )(*keep, *got)
    return list(outs[::2]), list(outs[1::2])


def by_plane_kernel(parts, *refs):
    first = 0
    for r in range(parts):
        keep, got = refs[r], refs[parts + r]
        last = first + keep.shape[2]
        for k, out in enumerate(refs[2 * parts :]):
            out[:, first:last] = (keep[k].astype(F32) + got[k].astype(F32)).astype(BF16)
        first = last


def by_plane(keep, got):
    parts = len(keep)
    planes = lax.axis_size("fsdp") // 2
    keep = [value.reshape(planes, -1, value.shape[2]) for value in keep]
    got = [value.reshape(planes, -1, value.shape[2]) for value in got]
    shape = (keep[0].shape[1], sum(value.shape[2] for value in keep))
    return pl.pallas_call(
        functools.partial(by_plane_kernel, parts),
        out_shape=[jax.ShapeDtypeStruct(shape, BF16)] * planes,
        in_specs=[pl.BlockSpec(memory_space=pltpu.VMEM)] * (2 * parts),
        out_specs=[pl.BlockSpec(memory_space=pltpu.VMEM)] * planes,
        compiler_params=pltpu.CompilerParams(vmem_limit_bytes=40 * 2**20),
        name="add_by_plane",
    )(*keep, *got)


def plane_step(keep, got, step):
    keep, sent = halve(keep, got)
    return keep, across_plane(sent, step)


def z_sends(sums):
    return [sums[0]] + [send_z(value, k) for k, value in enumerate(sums) if k > 0]


def summed(landed):
    return functools.reduce(jnp.add, [piece.astype(F32) for piece in landed]).astype(BF16)


def spread(mine):
    blocks = lax.axis_size("seq")
    pieces = [mine] + [send_seq(mine, j) for j in range(1, blocks)]
    here = lax.axis_index("seq")
    rows = []
    for i in range(blocks):
        row = pieces[0]
        for j in range(1, blocks):
            row = jnp.where((here ^ j) == i, pieces[j], row)
        rows.append(row)
    return jnp.concatenate(rows, axis=0).astype(F32)


def row_order(width):
    planes = lax.axis_size("fsdp") // 2
    blocks = lax.axis_size("seq")
    n = width // (planes * 2 * blocks)
    me = lax.axis_index("fsdp")
    r = lax.broadcasted_iota(jnp.int32, (1, width), 1)
    i = r % n
    k = (r // n) % planes
    j = (r // (n * planes)) % blocks
    c = r // (n * planes * blocks)
    f = (((me // 2) ^ k) * 2) + ((me % 2) ^ c)
    natural = (f * blocks + (lax.axis_index("seq") ^ j)) * n + i
    d = lax.broadcasted_iota(jnp.int32, (width, width), 0)
    return (d == natural).astype(BF16)


def normalized(field):
    centered = field - jnp.mean(field, axis=-1, keepdims=True)
    inverse = lax.rsqrt(jnp.mean(centered * centered, axis=-1, keepdims=True) + EPSILON)
    return centered * inverse, inverse


def norm_back(grad_normal, normal, inverse):
    return inverse * (
        grad_normal
        - jnp.mean(grad_normal, axis=-1, keepdims=True)
        - normal * jnp.mean(grad_normal * normal, axis=-1, keepdims=True)
    )


def rope_tables(positions, head_dim):
    half_dim = head_dim // 2
    frequency = 10000.0 ** (-(2.0 * jnp.arange(half_dim, dtype=F32)) / head_dim)
    angles = positions.astype(F32)[:, None] * frequency[None, :]
    cosine, sine = jnp.cos(angles), jnp.sin(angles)
    return (
        jnp.concatenate([cosine] * 4, axis=1),
        jnp.concatenate([-sine, sine, -sine, sine], axis=1),
    )


def turned(pair, head_dim):
    lane = lax.broadcasted_iota(jnp.int32, pair.shape, 1)
    wide = pair.shape[1]
    half_dim = head_dim // 2
    return jnp.where(
        lane % head_dim < half_dim,
        pltpu.roll(pair, wide - half_dim, 1),
        pltpu.roll(pair, half_dim, 1),
    )


def attention_kernel(
    head_dim,
    count,
    before_ref,
    inputs_ref,
    after_ref,
    cosine_ref,
    sine_ref,
    *refs,
):
    first_ref, queries_ref, keys_ref, values_ref, probs_ref, attended_ref = refs[count : count + 6]
    weight = whole_weight(refs[:count], refs[count + 6 :])
    row_count, width = inputs_ref.shape
    wide = row_count + 2 * HALF
    pair = 2 * head_dim
    rows = jnp.concatenate([before_ref[...], inputs_ref[...], after_ref[...]], axis=0)
    normal, _ = normalized(rows.astype(F32))
    first_wide = normal.astype(BF16)
    first_in = first_wide[HALF : HALF + row_count]
    first_ref[...] = first_wide
    cosine, sine = cosine_ref[...], sine_ref[...]
    own_cosine, own_sine = (t[HALF : HALF + row_count] for t in (cosine, sine))
    here = lax.axis_index("seq")
    length = row_count * lax.axis_size("seq")
    first_key = here * row_count - HALF
    row = lax.broadcasted_iota(jnp.int32, (row_count, wide), 0)
    column = lax.broadcasted_iota(jnp.int32, (row_count, wide), 1)
    distance = column - HALF - row
    key_pos = first_key + column
    allowed = (key_pos >= 0) & (key_pos < length) & (jnp.abs(distance) <= HALF)
    low_lanes = lax.broadcasted_iota(jnp.int32, (row_count, pair), 1) < head_dim

    mixed_q = dot(first_in, weight[:, :width])
    mixed_k = dot(first_wide, weight[:, width : 2 * width])
    values_ref[...] = dot(first_wide, weight[:, 2 * width :]).astype(BF16)
    for p in range(width // pair):
        lanes = slice(p * pair, (p + 1) * pair)
        q = mixed_q[:, lanes]
        k = mixed_k[:, lanes]
        q = (q * own_cosine + turned(q, head_dim) * own_sine).astype(BF16)
        q = (q.astype(F32) * head_dim**-0.5).astype(BF16)
        k = (k * cosine + turned(k, head_dim) * sine).astype(BF16)
        queries_ref[:, lanes] = q
        keys_ref[:, lanes] = k
        v = values_ref[:, lanes]
        heads = []
        for side in range(2):
            mine = low_lanes if side == 0 else ~low_lanes
            scores = dot(jnp.where(mine, q, jnp.zeros_like(q)), k, ((1,), (1,)))
            scores = jnp.where(allowed, scores, MASKED)
            row_max = jnp.max(scores, axis=-1, keepdims=True)
            exponents = jnp.exp(scores - row_max)
            row_sum = jnp.sum(exponents, axis=-1, keepdims=True)
            weights = (exponents / row_sum).astype(BF16)
            probs_ref[2 * p + side] = weights
            heads.append(dot(weights, v))
        attended_ref[:, lanes] = jnp.where(low_lanes, heads[0], heads[1]).astype(BF16)


def attention_forward(before, inputs, after, cosine, sine, pieces, head_dim):
    row_count, width = inputs.shape
    wide = row_count + 2 * HALF
    heads = width // head_dim
    shapes = (
        (wide, width),
        (row_count, width),
        (wide, width),
        (wide, width),
        (heads, row_count, wide),
        (row_count, width),
    )
    return pl.pallas_call(
        functools.partial(attention_kernel, head_dim, len(pieces)),
        out_shape=[jax.ShapeDtypeStruct(shape, BF16) for shape in shapes],
        in_specs=[pl.BlockSpec(memory_space=pltpu.VMEM)] * (5 + len(pieces)),
        out_specs=[pl.BlockSpec(memory_space=pltpu.VMEM)] * 6,
        scratch_shapes=weight_scratch(pieces),
        compiler_params=pltpu.CompilerParams(vmem_limit_bytes=40 * 2**20),
        name="attention_forward",
    )(before, inputs, after, cosine, sine, *pieces)


def mlp_kernel(count, inputs_ref, attended_ref, cotangent_ref, order_ref, *refs):
    outputs_ref, grad_middle_ref, grad_attended_ref = refs[count : count + 3]
    right_ref, own_left_ref, sent_left_ref = refs[count + 3 : count + 6]
    weight = whole_weight(refs[:count], refs[count + 6 :])
    width = inputs_ref.shape[1]
    hidden = (weight.shape[1] - width) // 3
    attn_out = slice(0, width)
    into = slice(width, width + 2 * hidden)
    back = slice(width + 2 * hidden, width + 3 * hidden)
    transposed = ((1,), (1,))
    attended = attended_ref[...]
    middle = inputs_ref[...].astype(F32) + dot(attended, weight[:, attn_out])
    normal, inverse = normalized(middle)
    second_in = normal.astype(BF16)
    gate_up = dot(second_in, weight[:, into])
    gate, up = gate_up[:, :hidden], gate_up[:, hidden:]
    slope = (2.0 / jnp.pi) ** 0.5
    square = gate * gate
    level = jnp.tanh(slope * (gate + 0.044715 * gate * square))
    activated = 0.5 * gate * (1.0 + level)
    steep = 0.5 * (1.0 + level) + 0.5 * gate * (1.0 - level * level) * slope * (
        1.0 + 3 * 0.044715 * square
    )
    product = (activated * up).astype(BF16)
    outputs_ref[...] = (middle + dot(product, weight[:, back], transposed)).astype(BF16)
    grad_out = cotangent_ref[...]
    grad_product = dot(grad_out, weight[:, back])
    grad_gate_up = jnp.concatenate(
        [grad_product * up * steep, grad_product * activated], axis=1
    ).astype(BF16)
    grad_normal = dot(grad_gate_up, weight[:, into], transposed)
    grad_middle = grad_out.astype(F32) + norm_back(grad_normal, normal, inverse)
    grad_middle_ref[...] = grad_middle
    grad_attn_low = grad_middle.astype(BF16)
    grad_attended_ref[...] = dot(grad_attn_low, weight[:, attn_out], transposed).astype(BF16)
    right_ref[:, attn_out] = grad_attn_low
    right_ref[:, into] = grad_gate_up
    right_ref[:, back] = product
    depth = width // 2
    for x, left in enumerate((attended, second_in, grad_out)):
        moved = dot(left, order_ref[...]).astype(BF16)
        own_left_ref[x] = moved[:, :depth]
        sent_left_ref[x] = moved[:, depth:]


def mlp_both_ways(inputs, attended, cotangent, order, pieces):
    row_count, width = inputs.shape
    shapes = (
        ((row_count, width), BF16),
        ((row_count, width), F32),
        ((row_count, width), BF16),
        ((row_count, pieces[0].shape[-1]), BF16),
        ((3, row_count, width // 2), BF16),
        ((3, row_count, width // 2), BF16),
    )
    return pl.pallas_call(
        functools.partial(mlp_kernel, len(pieces)),
        out_shape=[jax.ShapeDtypeStruct(*shape) for shape in shapes],
        in_specs=[pl.BlockSpec(memory_space=pltpu.VMEM)] * (4 + len(pieces)),
        out_specs=[pl.BlockSpec(memory_space=pltpu.VMEM)] * 6,
        scratch_shapes=weight_scratch(pieces),
        compiler_params=pltpu.CompilerParams(vmem_limit_bytes=48 * 2**20),
        name="mlp_both_ways",
    )(inputs, attended, cotangent, order, *pieces)


def attention_back_kernel(
    head_dim,
    grad_ref,
    probs_ref,
    queries_ref,
    keys_ref,
    values_ref,
    cosine_ref,
    sine_ref,
    grad_queries_ref,
    wide_ref,
    own_ref,
    low_ref,
    high_ref,
):
    row_count, width = grad_ref.shape
    pair = 2 * head_dim
    cosine, sine = cosine_ref[...], sine_ref[...]
    own_cosine, own_sine = (t[HALF : HALF + row_count] for t in (cosine, sine))
    low_lanes = lax.broadcasted_iota(jnp.int32, (row_count, pair), 1) < head_dim
    over_rows = ((0,), (0,))

    def put(field, lanes):
        rounded = field.astype(BF16)
        wide_ref[:, lanes] = rounded
        low_ref[:, lanes] = rounded[:HALF]
        own_ref[:, lanes] = field[HALF : HALF + row_count]
        high_ref[:, lanes] = rounded[HALF + row_count :]

    for p in range(width // pair):
        lanes = slice(p * pair, (p + 1) * pair)
        grad, q = grad_ref[:, lanes], queries_ref[:, lanes]
        k, v = keys_ref[:, lanes], values_ref[:, lanes]
        grad_q, grad_k, grad_v = [], 0.0, 0.0
        for side in range(2):
            mine = low_lanes if side == 0 else ~low_lanes
            weights_low = probs_ref[2 * p + side]
            weights = weights_low.astype(F32)
            grad_mine = jnp.where(mine, grad, jnp.zeros_like(grad))
            q_mine = jnp.where(mine, q, jnp.zeros_like(q))
            grad_probs = dot(grad_mine, v, ((1,), (1,)))
            weighted = weights * grad_probs
            grad_scores = (
                weighted - weights * jnp.sum(weighted, axis=-1, keepdims=True)
            ).astype(BF16)
            grad_q.append(dot(grad_scores, k))
            grad_k = grad_k + dot(grad_scores, q_mine, over_rows)
            grad_v = grad_v + dot(weights_low, grad_mine, over_rows)
        turn = jnp.where(low_lanes, grad_q[0], grad_q[1]) * head_dim**-0.5
        grad_queries_ref[:, lanes] = (
            turn * own_cosine - turned(turn, head_dim) * own_sine
        ).astype(BF16)
        put(grad_k * cosine - turned(grad_k, head_dim) * sine, lanes)
        put(grad_v, slice(width + p * pair, width + (p + 1) * pair))


def attention_backward(grad, probs, queries, keys, values, cosine, sine, head_dim):
    row_count, width = grad.shape
    shapes = (
        ((row_count, width), BF16),
        ((row_count + 2 * HALF, 2 * width), BF16),
        ((row_count, 2 * width), F32),
        ((HALF, 2 * width), BF16),
        ((HALF, 2 * width), BF16),
    )
    return pl.pallas_call(
        functools.partial(attention_back_kernel, head_dim),
        out_shape=[jax.ShapeDtypeStruct(*shape) for shape in shapes],
        in_specs=[pl.BlockSpec(memory_space=pltpu.VMEM)] * 7,
        out_specs=[pl.BlockSpec(memory_space=pltpu.VMEM)] * len(shapes),
        compiler_params=pltpu.CompilerParams(vmem_limit_bytes=40 * 2**20),
        name="attention_backward",
    )(grad, probs, queries, keys, values, cosine, sine)


def input_grads_kernel(
    count, grad_queries_ref, own_ref, below_ref, above_ref, inputs_ref, middle_ref, *refs
):
    out_ref = refs[count]
    weight = whole_weight(refs[:count], refs[count + 1 :])
    row_count, width = inputs_ref.shape
    below, above = below_ref[...].astype(F32), above_ref[...].astype(F32)
    inner = jnp.zeros((row_count - HALF, below.shape[1]), F32)
    grad_kv = own_ref[...] + jnp.concatenate([below, inner]) + jnp.concatenate([inner, above])
    normal, inverse = normalized(inputs_ref[...].astype(F32))
    transposed = ((1,), (1,))
    grad_normal = dot(grad_queries_ref[...], weight[:, :width], transposed) + dot(
        grad_kv.astype(BF16), weight[:, width:], transposed
    )
    out_ref[...] = middle_ref[...] + norm_back(grad_normal, normal, inverse)


def input_grads(grad_queries, own, below, above, inputs, grad_middle, pieces):
    return pl.pallas_call(
        functools.partial(input_grads_kernel, len(pieces)),
        out_shape=jax.ShapeDtypeStruct(inputs.shape, F32),
        in_specs=[pl.BlockSpec(memory_space=pltpu.VMEM)] * (6 + len(pieces)),
        out_specs=pl.BlockSpec(memory_space=pltpu.VMEM),
        scratch_shapes=weight_scratch(pieces),
        compiler_params=pltpu.CompilerParams(vmem_limit_bytes=40 * 2**20),
        name="input_grads",
    )(grad_queries, own, below, above, inputs, grad_middle, *pieces)


def on_device(tokens, cotangent, w_qkv, w_attn_out, w_in, w_mlp_out, gain_attn, gain_mlp):
    row_count = tokens.shape[1]
    width = tokens.shape[2]
    head_dim = width // HEADS
    hidden = w_mlp_out.shape[0]
    blocks = lax.axis_size("seq")
    here = lax.axis_index("seq")
    n = w_qkv.shape[0] // blocks

    together = lax.optimization_barrier

    gain_one = gain_attn.astype(F32)[:, None]
    gain_two = gain_mlp.astype(F32)[:, None]

    def quarter(value):
        return lax.dynamic_slice_in_dim(value, here * n, n, 0)

    inputs_low = tokens[0]
    mine = (quarter(w_qkv).astype(F32) * quarter(gain_one)).astype(BF16)
    along = along_z(mine)
    order = row_order(width)
    key_pos = here * row_count - HALF + jnp.arange(row_count + 2 * HALF, dtype=jnp.int32)
    cosine, sine = rope_tables(key_pos, head_dim)
    before = send_along(inputs_low[row_count - HALF :], 1)
    after = send_along(inputs_low[:HALF], -1)
    along, before, after = together((along, before, after))
    held = by_range(along)
    got = across_plane(held, 0)
    rest = jnp.concatenate(
        [w_attn_out, (w_in.astype(F32) * gain_two).astype(BF16), w_mlp_out.T], axis=1
    )
    mine_rest, _ = together((quarter(rest), along))
    along_rest = along_z(mine_rest)
    across = across_rest_of_plane(held, got)

    own = (w_qkv.astype(F32) * gain_one).astype(BF16).reshape(blocks, n, -1)
    own, rest, along_rest, across = together((own, rest, along_rest, across))
    across, cosine, sine, order = together((across, cosine, sine, order))
    held_rest = by_range(along_rest)
    got_rest = across_plane(held_rest, 0)
    qkv_pieces = with_other_core([own] + across)
    first_wide, queries, keys, values, probs, attended = attention_forward(
        before, inputs_low, after, cosine, sine, qkv_pieces, head_dim
    )
    across_rest = across_rest_of_plane(held_rest, got_rest)
    rest_pieces = with_other_core([rest.reshape(blocks, n, -1)] + across_rest)
    outputs, grad_middle, grad_attended, right, own_left, sent_left = mlp_both_ways(
        inputs_low, attended, cotangent[0], order, rest_pieces
    )
    other_left, other_right = send_core(sent_left), send_core(right)
    moved = dot(first_wide, order).astype(BF16)
    own_first, sent_first = moved[None, :, : width // 2], moved[None, :, width // 2 :]
    other_first = send_core(sent_first)
    grad_queries, grad_wide, grad_own, grad_low, grad_high = attention_backward(
        grad_attended, probs, queries, keys, values, cosine, sine, head_dim
    )
    own_left, _ = together((own_left, grad_wide))
    products, first = [], 0
    for x, columns in enumerate((width, 2 * hidden, hidden)):
        products.append((0, x, 0, row_count, 0, first, columns))
        first += columns
    keep_rest, sent_rest = partial_grads(
        [own_left], [other_left], [right], [other_right], products
    )
    got_rest = across_plane(sent_rest, 0)
    wide = row_count + 2 * HALF
    products = [
        (0, 0, HALF, row_count, 0, 0, width),
        (0, 0, 0, wide, 1, 0, 2 * width),
    ]
    own_first, _ = together((own_first, keep_rest))
    keep_qkv, sent_qkv = partial_grads(
        [own_first],
        [other_first],
        [grad_queries, grad_wide],
        [send_core(grad_queries), send_core(grad_wide)],
        products,
    )
    grad_low, grad_high, _ = together((grad_low, grad_high, keep_qkv))
    above = send_along(grad_low, -1)
    below = send_along(grad_high, 1)
    got_rest, _ = together((got_rest, keep_qkv))
    begun = []
    for step in range(1, bits_of(blocks)):
        keep_rest, sent = halve(keep_rest, got_rest)
        begun.append(sent)
        got_rest = across_plane(sent, step)
    sent_qkv, _ = together((sent_qkv, begun))
    got_qkv = across_plane(sent_qkv, 0)
    sums_rest = by_plane(keep_rest, got_rest)
    landed_rest = z_sends(sums_rest)
    for step in range(1, bits_of(blocks)):
        keep_qkv, got_qkv = plane_step(keep_qkv, got_qkv, step)
    above, below, _ = together((above, below, keep_qkv))
    sums_qkv = by_plane(keep_qkv, got_qkv)
    landed_qkv = z_sends(sums_qkv)
    mine_rest = summed(landed_rest)
    mine_qkv = summed(landed_qkv)
    grad_inputs = input_grads(
        grad_queries, grad_own, below, above, inputs_low, grad_middle, qkv_pieces
    )
    sum_rest = spread(mine_rest)
    sum_qkv = spread(mine_qkv)
    sum_attn_out = sum_rest[:, :width]
    sum_in = sum_rest[:, width : width + 2 * hidden]
    sum_mlp = sum_rest[:, width + 2 * hidden :]
    return (
        outputs[None],
        grad_inputs[None],
        sum_qkv * gain_one,
        sum_attn_out,
        sum_in * gain_two,
        sum_mlp.T,
        jnp.sum(sum_qkv * w_qkv.astype(F32), axis=1),
        jnp.sum(sum_in * w_in.astype(F32), axis=1),
    )


def solution(mesh):
    in_specs = (
        P("fsdp", "seq", None),
        P("fsdp", "seq", None),
        P("fsdp", None),
        P("fsdp", None),
        P("fsdp", None),
        P(None, "fsdp"),
        P("fsdp"),
        P("fsdp"),
    )
    out_specs = (
        P("fsdp", "seq", None),
        P("fsdp", "seq", None),
        P("fsdp", None),
        P("fsdp", None),
        P("fsdp", None),
        P(None, "fsdp"),
        P("fsdp"),
        P("fsdp"),
    )
    return jax.shard_map(
        on_device, mesh=mesh, in_specs=in_specs, out_specs=out_specs, check_vma=False
    )
```

```python
import functools

import jax
import jax.numpy as jnp
from jax import lax
from jax.experimental import pallas as pl
from jax.experimental.pallas import tpu as pltpu
from jax.sharding import PartitionSpec as P

HEADS = 12
HALF = 64
EPSILON = 1e-05
MASKED = -1e30
F32 = jnp.float32
BF16 = jnp.bfloat16


def dot(a, b, dims=((1,), (0,))):
    return lax.dot_general(a, b, (dims, ((), ())), preferred_element_type=F32)


def send_core(value):
    count = lax.axis_size("fsdp")
    return lax.ppermute(value, "fsdp", [(i, i ^ 1) for i in range(count)])


def send_z(value, step):
    count = lax.axis_size("fsdp")
    return lax.ppermute(value, "fsdp", [(i, i ^ (2 * step)) for i in range(count)])


def send_seq(value, step):
    count = lax.axis_size("seq")
    return lax.ppermute(value, "seq", [(i, i ^ step) for i in range(count)])


def send_along(value, step):
    count = lax.axis_size("seq")
    first, last = (max(0, -step), min(count, count - step))
    return lax.ppermute(value, "seq", [(i, i + step) for i in range(first, last)])


def bits_of(count):
    return count.bit_length() - 1


def column_cuts(width):
    parts = bits_of(lax.axis_size("seq"))
    tiles = width // 128
    edges = [(2 * r * tiles + parts) // (2 * parts) * 128 for r in range(parts)] + [width]
    return list(zip(edges[:-1], edges[1:]))


def direction(part, step):
    return 1 << ((part + step) % bits_of(lax.axis_size("seq")))


def along_z(mine):
    planes = lax.axis_size("fsdp") // 2
    return [send_z(mine, k) for k in range(1, planes)]


def by_range(along):
    return [
        jnp.stack([piece[:, first:last] for piece in along])
        for first, last in column_cuts(along[0].shape[1])
    ]


def across_plane(held, step):
    return [send_seq(value, direction(r, step)) for r, value in enumerate(held)]


def joined_ranges(held, got):
    return [jnp.concatenate(pair) for pair in zip(held, got)]


def across_rest_of_plane(held, got):
    for step in range(1, bits_of(lax.axis_size("seq"))):
        held = joined_ranges(held, got)
        got = across_plane(held, step)
    return held + got


def distances(part):
    found = [0]
    for step in range(bits_of(lax.axis_size("seq"))):
        found = found + [j ^ direction(part, step) for j in found]
    return found


def fits(n):
    return n % 8 == 0


def with_other_core(pieces):
    pieces = pieces + [send_core(piece) for piece in pieces]
    if fits(pieces[0].shape[1]):
        return pieces
    whole = sum(piece.size for piece in pieces)
    blocks, n, width = pieces[0].shape
    out = jnp.zeros((whole // (n * width), n, width), BF16)
    for to, first, last, source, index in placements(pieces, n, width):
        block = lax.dynamic_slice_in_dim(source, index, 1, 0)
        out = lax.dynamic_update_slice(out, block, (to, 0, first))
    return [out.reshape(-1, width)]


def placements(pieces, n, width):
    planes = lax.axis_size("fsdp") // 2
    blocks = lax.axis_size("seq")
    me, here = lax.axis_index("fsdp"), lax.axis_index("seq")
    plane, core = me // 2, me % 2
    half = len(pieces) // 2
    cuts = column_cuts(width)
    found = []
    for side in range(2):
        parity = core ^ side
        own, *others = pieces[side * half : (side + 1) * half]
        for j in range(blocks):
            found.append(((plane * 2 + parity) * blocks + j, 0, width, own, j))
        for r, (first, last) in enumerate(cuts):
            reach = distances(r)
            for m, j in enumerate(reach):
                late = m >= blocks // 2
                source = others[r + late * len(cuts)]
                for k in range(1, planes):
                    to = ((plane ^ k) * 2 + parity) * blocks + (here ^ j)
                    index = (m % (blocks // 2)) * (planes - 1) + k - 1
                    found.append((to, first, last, source, index))
    return found


def weight_scratch(pieces):
    if len(pieces) == 1:
        return []
    blocks, n, width = pieces[0].shape
    return [pltpu.VMEM((lax.axis_size("fsdp") * blocks, n, width), BF16)]


def whole_weight(sources, scratch):
    if not scratch:
        return sources[0][...]
    (out,) = scratch
    _, n, width = out.shape
    for to, first, last, source, index in placements(sources, n, width):
        out[to, :, first:last] = source[index]
    return out[...].reshape(-1, width)


def grads_kernel(counts, products, *refs):
    lefts, rights = counts
    own_a, other_a = refs[:lefts], refs[lefts : 2 * lefts]
    refs = refs[2 * lefts :]
    own_b, other_b = refs[:rights], refs[rights : 2 * rights]
    outs = refs[2 * rights :]
    blocks = lax.axis_size("seq")
    cuts = column_cuts(sum(product[-1] for product in products))
    start = 0
    for left, index, row, count, right, column, width in products:
        reach = slice(row, row + count)
        left_own, left_other = own_a[left][index, reach].T, other_a[left][index, reach].T
        rows = left_own.shape[0] // blocks
        for r, (low, high) in enumerate(cuts):
            keep, sent = outs[2 * r], outs[2 * r + 1]
            for first in range(max(low, start), min(high, start + width), 512):
                last = min(first + 512, high, start + width)
                lanes = slice(column + first - start, column + last - start)
                total = dot(left_own, own_b[right][:, lanes]) + dot(
                    left_other, other_b[right][:, lanes]
                )
                for m, j in enumerate(halving_order(r)):
                    out = sent if m >= blocks // 2 else keep
                    out[m % (blocks // 2), :, first - low : last - low] = total[
                        j * rows : (j + 1) * rows
                    ].astype(BF16)
        start += width


def halving_order(part):
    steps = bits_of(lax.axis_size("seq"))
    return [
        sum(direction(part, t) for t in range(steps) if m >> (steps - 1 - t) & 1)
        for m in range(1 << steps)
    ]


def partial_grads(own_a, other_a, own_b, other_b, products):
    blocks = lax.axis_size("seq")
    rows = own_a[0].shape[2] // blocks
    shapes = [
        jax.ShapeDtypeStruct((blocks // 2, rows, last - first), BF16)
        for first, last in column_cuts(sum(product[-1] for product in products))
        for _ in range(2)
    ]
    operands = [*own_a, *other_a, *own_b, *other_b]
    outs = pl.pallas_call(
        functools.partial(grads_kernel, (len(own_a), len(own_b)), products),
        out_shape=shapes,
        in_specs=[pl.BlockSpec(memory_space=pltpu.VMEM)] * len(operands),
        out_specs=[pl.BlockSpec(memory_space=pltpu.VMEM)] * len(shapes),
        compiler_params=pltpu.CompilerParams(vmem_limit_bytes=40 * 2**20),
        name="weight_grads",
    )(*operands)
    return list(outs[::2]), list(outs[1::2])


def halve_kernel(parts, *refs):
    for r in range(parts):
        keep, got = refs[r], refs[parts + r]
        low, high = refs[2 * parts + 2 * r], refs[2 * parts + 2 * r + 1]
        half = low.shape[0]
        low[...] = (keep[:half].astype(F32) + got[:half].astype(F32)).astype(BF16)
        high[...] = (keep[half:].astype(F32) + got[half:].astype(F32)).astype(BF16)


def halve(keep, got):
    parts = len(keep)
    shapes = [
        jax.ShapeDtypeStruct((value.shape[0] // 2,) + value.shape[1:], BF16)
        for value in keep
        for _ in range(2)
    ]
    outs = pl.pallas_call(
        functools.partial(halve_kernel, parts),
        out_shape=shapes,
        in_specs=[pl.BlockSpec(memory_space=pltpu.VMEM)] * (2 * parts),
        out_specs=[pl.BlockSpec(memory_space=pltpu.VMEM)] * (2 * parts),
        compiler_params=pltpu.CompilerParams(vmem_limit_bytes=40 * 2**20),
        name="add_and_halve",
    )(*keep, *got)
    return list(outs[::2]), list(outs[1::2])


def by_plane_kernel(parts, *refs):
    first = 0
    for r in range(parts):
        keep, got = refs[r], refs[parts + r]
        last = first + keep.shape[2]
        for k, out in enumerate(refs[2 * parts :]):
            out[:, first:last] = (keep[k].astype(F32) + got[k].astype(F32)).astype(BF16)
        first = last


def by_plane(keep, got):
    parts = len(keep)
    planes = lax.axis_size("fsdp") // 2
    keep = [value.reshape(planes, -1, value.shape[2]) for value in keep]
    got = [value.reshape(planes, -1, value.shape[2]) for value in got]
    shape = (keep[0].shape[1], sum(value.shape[2] for value in keep))
    return pl.pallas_call(
        functools.partial(by_plane_kernel, parts),
        out_shape=[jax.ShapeDtypeStruct(shape, BF16)] * planes,
        in_specs=[pl.BlockSpec(memory_space=pltpu.VMEM)] * (2 * parts),
        out_specs=[pl.BlockSpec(memory_space=pltpu.VMEM)] * planes,
        compiler_params=pltpu.CompilerParams(vmem_limit_bytes=40 * 2**20),
        name="add_by_plane",
    )(*keep, *got)


def plane_step(keep, got, step):
    keep, sent = halve(keep, got)
    return keep, across_plane(sent, step)


def z_sends(sums):
    return [sums[0]] + [send_z(value, k) for k, value in enumerate(sums) if k > 0]


def summed(landed):
    return functools.reduce(jnp.add, [piece.astype(F32) for piece in landed]).astype(BF16)


def spread(mine):
    blocks = lax.axis_size("seq")
    pieces = [mine] + [send_seq(mine, j) for j in range(1, blocks)]
    here = lax.axis_index("seq")
    rows = []
    for i in range(blocks):
        row = pieces[0]
        for j in range(1, blocks):
            row = jnp.where((here ^ j) == i, pieces[j], row)
        rows.append(row)
    return jnp.concatenate(rows, axis=0).astype(F32)


def row_order(width):
    planes = lax.axis_size("fsdp") // 2
    blocks = lax.axis_size("seq")
    n = width // (planes * 2 * blocks)
    me = lax.axis_index("fsdp")
    r = lax.broadcasted_iota(jnp.int32, (1, width), 1)
    i = r % n
    k = (r // n) % planes
    j = (r // (n * planes)) % blocks
    c = r // (n * planes * blocks)
    f = (((me // 2) ^ k) * 2) + ((me % 2) ^ c)
    natural = (f * blocks + (lax.axis_index("seq") ^ j)) * n + i
    d = lax.broadcasted_iota(jnp.int32, (width, width), 0)
    return (d == natural).astype(BF16)


def normalized(field):
    centered = field - jnp.mean(field, axis=-1, keepdims=True)
    inverse = lax.rsqrt(jnp.mean(centered * centered, axis=-1, keepdims=True) + EPSILON)
    return centered * inverse, inverse


def norm_back(grad_normal, normal, inverse):
    return inverse * (
        grad_normal
        - jnp.mean(grad_normal, axis=-1, keepdims=True)
        - normal * jnp.mean(grad_normal * normal, axis=-1, keepdims=True)
    )


def rope_tables(positions, head_dim):
    half_dim = head_dim // 2
    frequency = 10000.0 ** (-(2.0 * jnp.arange(half_dim, dtype=F32)) / head_dim)
    angles = positions.astype(F32)[:, None] * frequency[None, :]
    cosine, sine = jnp.cos(angles), jnp.sin(angles)
    return (
        jnp.concatenate([cosine] * 4, axis=1),
        jnp.concatenate([-sine, sine, -sine, sine], axis=1),
    )


def turned(pair, head_dim):
    lane = lax.broadcasted_iota(jnp.int32, pair.shape, 1)
    wide = pair.shape[1]
    half_dim = head_dim // 2
    return jnp.where(
        lane % head_dim < half_dim,
        pltpu.roll(pair, wide - half_dim, 1),
        pltpu.roll(pair, half_dim, 1),
    )


def attention_kernel(
    head_dim,
    count,
    before_ref,
    inputs_ref,
    after_ref,
    cosine_ref,
    sine_ref,
    *refs,
):
    first_ref, queries_ref, keys_ref, values_ref, probs_ref, attended_ref = refs[count : count + 6]
    weight = whole_weight(refs[:count], refs[count + 6 :])
    row_count, width = inputs_ref.shape
    wide = row_count + 2 * HALF
    pair = 2 * head_dim
    rows = jnp.concatenate([before_ref[...], inputs_ref[...], after_ref[...]], axis=0)
    normal, _ = normalized(rows.astype(F32))
    first_wide = normal.astype(BF16)
    first_in = first_wide[HALF : HALF + row_count]
    first_ref[...] = first_wide
    cosine, sine = cosine_ref[...], sine_ref[...]
    own_cosine, own_sine = (t[HALF : HALF + row_count] for t in (cosine, sine))
    here = lax.axis_index("seq")
    length = row_count * lax.axis_size("seq")
    first_key = here * row_count - HALF
    row = lax.broadcasted_iota(jnp.int32, (row_count, wide), 0)
    column = lax.broadcasted_iota(jnp.int32, (row_count, wide), 1)
    distance = column - HALF - row
    key_pos = first_key + column
    allowed = (key_pos >= 0) & (key_pos < length) & (jnp.abs(distance) <= HALF)
    low_lanes = lax.broadcasted_iota(jnp.int32, (row_count, pair), 1) < head_dim

    mixed_q = dot(first_in, weight[:, :width])
    mixed_k = dot(first_wide, weight[:, width : 2 * width])
    values_ref[...] = dot(first_wide, weight[:, 2 * width :]).astype(BF16)
    for p in range(width // pair):
        lanes = slice(p * pair, (p + 1) * pair)
        q = mixed_q[:, lanes]
        k = mixed_k[:, lanes]
        q = (q * own_cosine + turned(q, head_dim) * own_sine).astype(BF16)
        q = (q.astype(F32) * head_dim**-0.5).astype(BF16)
        k = (k * cosine + turned(k, head_dim) * sine).astype(BF16)
        queries_ref[:, lanes] = q
        keys_ref[:, lanes] = k
        v = values_ref[:, lanes]
        heads = []
        for side in range(2):
            mine = low_lanes if side == 0 else ~low_lanes
            scores = dot(jnp.where(mine, q, jnp.zeros_like(q)), k, ((1,), (1,)))
            scores = jnp.where(allowed, scores, MASKED)
            row_max = jnp.max(scores, axis=-1, keepdims=True)
            exponents = jnp.exp(scores - row_max)
            row_sum = jnp.sum(exponents, axis=-1, keepdims=True)
            weights = (exponents / row_sum).astype(BF16)
            probs_ref[2 * p + side] = weights
            heads.append(dot(weights, v))
        attended_ref[:, lanes] = jnp.where(low_lanes, heads[0], heads[1]).astype(BF16)


def attention_forward(before, inputs, after, cosine, sine, pieces, head_dim):
    row_count, width = inputs.shape
    wide = row_count + 2 * HALF
    heads = width // head_dim
    shapes = (
        (wide, width),
        (row_count, width),
        (wide, width),
        (wide, width),
        (heads, row_count, wide),
        (row_count, width),
    )
    return pl.pallas_call(
        functools.partial(attention_kernel, head_dim, len(pieces)),
        out_shape=[jax.ShapeDtypeStruct(shape, BF16) for shape in shapes],
        in_specs=[pl.BlockSpec(memory_space=pltpu.VMEM)] * (5 + len(pieces)),
        out_specs=[pl.BlockSpec(memory_space=pltpu.VMEM)] * 6,
        scratch_shapes=weight_scratch(pieces),
        compiler_params=pltpu.CompilerParams(vmem_limit_bytes=40 * 2**20),
        name="attention_forward",
    )(before, inputs, after, cosine, sine, *pieces)


def mlp_kernel(count, inputs_ref, attended_ref, cotangent_ref, order_ref, *refs):
    outputs_ref, grad_middle_ref, grad_attended_ref = refs[count : count + 3]
    right_ref, own_left_ref, sent_left_ref = refs[count + 3 : count + 6]
    weight = whole_weight(refs[:count], refs[count + 6 :])
    width = inputs_ref.shape[1]
    hidden = (weight.shape[1] - width) // 3
    attn_out = slice(0, width)
    into = slice(width, width + 2 * hidden)
    back = slice(width + 2 * hidden, width + 3 * hidden)
    transposed = ((1,), (1,))
    attended = attended_ref[...]
    middle = inputs_ref[...].astype(F32) + dot(attended, weight[:, attn_out])
    normal, inverse = normalized(middle)
    second_in = normal.astype(BF16)
    gate_up = dot(second_in, weight[:, into])
    gate, up = gate_up[:, :hidden], gate_up[:, hidden:]
    slope = (2.0 / jnp.pi) ** 0.5
    square = gate * gate
    level = jnp.tanh(slope * (gate + 0.044715 * gate * square))
    activated = 0.5 * gate * (1.0 + level)
    steep = 0.5 * (1.0 + level) + 0.5 * gate * (1.0 - level * level) * slope * (
        1.0 + 3 * 0.044715 * square
    )
    product = (activated * up).astype(BF16)
    outputs_ref[...] = (middle + dot(product, weight[:, back], transposed)).astype(BF16)
    grad_out = cotangent_ref[...]
    grad_product = dot(grad_out, weight[:, back])
    grad_gate_up = jnp.concatenate(
        [grad_product * up * steep, grad_product * activated], axis=1
    ).astype(BF16)
    grad_normal = dot(grad_gate_up, weight[:, into], transposed)
    grad_middle = grad_out.astype(F32) + norm_back(grad_normal, normal, inverse)
    grad_middle_ref[...] = grad_middle
    grad_attn_low = grad_middle.astype(BF16)
    grad_attended_ref[...] = dot(grad_attn_low, weight[:, attn_out], transposed).astype(BF16)
    right_ref[:, attn_out] = grad_attn_low
    right_ref[:, into] = grad_gate_up
    right_ref[:, back] = product
    depth = width // 2
    for x, left in enumerate((attended, second_in, grad_out)):
        moved = dot(left, order_ref[...]).astype(BF16)
        own_left_ref[x] = moved[:, :depth]
        sent_left_ref[x] = moved[:, depth:]


def mlp_both_ways(inputs, attended, cotangent, order, pieces):
    row_count, width = inputs.shape
    shapes = (
        ((row_count, width), BF16),
        ((row_count, width), F32),
        ((row_count, width), BF16),
        ((row_count, pieces[0].shape[-1]), BF16),
        ((3, row_count, width // 2), BF16),
        ((3, row_count, width // 2), BF16),
    )
    return pl.pallas_call(
        functools.partial(mlp_kernel, len(pieces)),
        out_shape=[jax.ShapeDtypeStruct(*shape) for shape in shapes],
        in_specs=[pl.BlockSpec(memory_space=pltpu.VMEM)] * (4 + len(pieces)),
        out_specs=[pl.BlockSpec(memory_space=pltpu.VMEM)] * 6,
        scratch_shapes=weight_scratch(pieces),
        compiler_params=pltpu.CompilerParams(vmem_limit_bytes=48 * 2**20),
        name="mlp_both_ways",
    )(inputs, attended, cotangent, order, *pieces)


def attention_back_kernel(
    head_dim,
    grad_ref,
    probs_ref,
    queries_ref,
    keys_ref,
    values_ref,
    cosine_ref,
    sine_ref,
    grad_queries_ref,
    wide_ref,
    own_ref,
    low_ref,
    high_ref,
):
    row_count, width = grad_ref.shape
    pair = 2 * head_dim
    cosine, sine = cosine_ref[...], sine_ref[...]
    own_cosine, own_sine = (t[HALF : HALF + row_count] for t in (cosine, sine))
    low_lanes = lax.broadcasted_iota(jnp.int32, (row_count, pair), 1) < head_dim
    over_rows = ((0,), (0,))

    def put(field, lanes):
        rounded = field.astype(BF16)
        wide_ref[:, lanes] = rounded
        low_ref[:, lanes] = rounded[:HALF]
        own_ref[:, lanes] = field[HALF : HALF + row_count]
        high_ref[:, lanes] = rounded[HALF + row_count :]

    for p in range(width // pair):
        lanes = slice(p * pair, (p + 1) * pair)
        grad, q = grad_ref[:, lanes], queries_ref[:, lanes]
        k, v = keys_ref[:, lanes], values_ref[:, lanes]
        grad_q, grad_k, grad_v = [], 0.0, 0.0
        for side in range(2):
            mine = low_lanes if side == 0 else ~low_lanes
            weights_low = probs_ref[2 * p + side]
            weights = weights_low.astype(F32)
            grad_mine = jnp.where(mine, grad, jnp.zeros_like(grad))
            q_mine = jnp.where(mine, q, jnp.zeros_like(q))
            grad_probs = dot(grad_mine, v, ((1,), (1,)))
            weighted = weights * grad_probs
            grad_scores = (
                weighted - weights * jnp.sum(weighted, axis=-1, keepdims=True)
            ).astype(BF16)
            grad_q.append(dot(grad_scores, k))
            grad_k = grad_k + dot(grad_scores, q_mine, over_rows)
            grad_v = grad_v + dot(weights_low, grad_mine, over_rows)
        turn = jnp.where(low_lanes, grad_q[0], grad_q[1]) * head_dim**-0.5
        grad_queries_ref[:, lanes] = (
            turn * own_cosine - turned(turn, head_dim) * own_sine
        ).astype(BF16)
        put(grad_k * cosine - turned(grad_k, head_dim) * sine, lanes)
        put(grad_v, slice(width + p * pair, width + (p + 1) * pair))


def attention_backward(grad, probs, queries, keys, values, cosine, sine, head_dim):
    row_count, width = grad.shape
    shapes = (
        ((row_count, width), BF16),
        ((row_count + 2 * HALF, 2 * width), BF16),
        ((row_count, 2 * width), F32),
        ((HALF, 2 * width), BF16),
        ((HALF, 2 * width), BF16),
    )
    return pl.pallas_call(
        functools.partial(attention_back_kernel, head_dim),
        out_shape=[jax.ShapeDtypeStruct(*shape) for shape in shapes],
        in_specs=[pl.BlockSpec(memory_space=pltpu.VMEM)] * 7,
        out_specs=[pl.BlockSpec(memory_space=pltpu.VMEM)] * len(shapes),
        compiler_params=pltpu.CompilerParams(vmem_limit_bytes=40 * 2**20),
        name="attention_backward",
    )(grad, probs, queries, keys, values, cosine, sine)


def input_grads_kernel(
    count, grad_queries_ref, own_ref, below_ref, above_ref, inputs_ref, middle_ref, *refs
):
    out_ref = refs[count]
    weight = whole_weight(refs[:count], refs[count + 1 :])
    row_count, width = inputs_ref.shape
    below, above = below_ref[...].astype(F32), above_ref[...].astype(F32)
    inner = jnp.zeros((row_count - HALF, below.shape[1]), F32)
    grad_kv = own_ref[...] + jnp.concatenate([below, inner]) + jnp.concatenate([inner, above])
    normal, inverse = normalized(inputs_ref[...].astype(F32))
    transposed = ((1,), (1,))
    grad_normal = dot(grad_queries_ref[...], weight[:, :width], transposed) + dot(
        grad_kv.astype(BF16), weight[:, width:], transposed
    )
    out_ref[...] = middle_ref[...] + norm_back(grad_normal, normal, inverse)


def input_grads(grad_queries, own, below, above, inputs, grad_middle, pieces):
    return pl.pallas_call(
        functools.partial(input_grads_kernel, len(pieces)),
        out_shape=jax.ShapeDtypeStruct(inputs.shape, F32),
        in_specs=[pl.BlockSpec(memory_space=pltpu.VMEM)] * (6 + len(pieces)),
        out_specs=pl.BlockSpec(memory_space=pltpu.VMEM),
        scratch_shapes=weight_scratch(pieces),
        compiler_params=pltpu.CompilerParams(vmem_limit_bytes=60 * 2**20),
        name="input_grads",
    )(grad_queries, own, below, above, inputs, grad_middle, *pieces)


def on_device(tokens, cotangent, w_qkv, w_attn_out, w_in, w_mlp_out, gain_attn, gain_mlp):
    row_count = tokens.shape[1]
    width = tokens.shape[2]
    head_dim = width // HEADS
    hidden = w_mlp_out.shape[0]
    blocks = lax.axis_size("seq")
    here = lax.axis_index("seq")
    n = w_qkv.shape[0] // blocks

    together = lax.optimization_barrier

    gain_one = gain_attn.astype(F32)[:, None]
    gain_two = gain_mlp.astype(F32)[:, None]

    def quarter(value):
        return lax.dynamic_slice_in_dim(value, here * n, n, 0)

    inputs_low = tokens[0]
    mine = (quarter(w_qkv).astype(F32) * quarter(gain_one)).astype(BF16)
    along = along_z(mine)
    order = row_order(width)
    key_pos = here * row_count - HALF + jnp.arange(row_count + 2 * HALF, dtype=jnp.int32)
    cosine, sine = rope_tables(key_pos, head_dim)
    before = send_along(inputs_low[row_count - HALF :], 1)
    after = send_along(inputs_low[:HALF], -1)
    along, before, after = together((along, before, after))
    held = by_range(along)
    got = across_plane(held, 0)
    rest = jnp.concatenate(
        [w_attn_out, (w_in.astype(F32) * gain_two).astype(BF16), w_mlp_out.T], axis=1
    )
    mine_rest, _ = together((quarter(rest), along))
    along_rest = along_z(mine_rest)
    across = across_rest_of_plane(held, got)

    own = (w_qkv.astype(F32) * gain_one).astype(BF16).reshape(blocks, n, -1)
    across, cosine, sine, order = together((across, cosine, sine, order))
    held_rest = by_range(along_rest)
    got_rest = across_plane(held_rest, 0)
    qkv_pieces = with_other_core([own] + across)
    first_wide, queries, keys, values, probs, attended = attention_forward(
        before, inputs_low, after, cosine, sine, qkv_pieces, head_dim
    )
    across_rest = across_rest_of_plane(held_rest, got_rest)
    rest_pieces = with_other_core([rest.reshape(blocks, n, -1)] + across_rest)
    outputs, grad_middle, grad_attended, right, own_left, sent_left = mlp_both_ways(
        inputs_low, attended, cotangent[0], order, rest_pieces
    )
    other_left, other_right = send_core(sent_left), send_core(right)
    moved = dot(first_wide, order).astype(BF16)
    own_first, sent_first = moved[None, :, : width // 2], moved[None, :, width // 2 :]
    other_first = send_core(sent_first)
    grad_queries, grad_wide, grad_own, grad_low, grad_high = attention_backward(
        grad_attended, probs, queries, keys, values, cosine, sine, head_dim
    )
    wide = row_count + 2 * HALF
    parts = {
        "attn_out": [(0, 0, 0, row_count, 0, 0, width)],
        "in": [(0, 1, 0, row_count, 0, width, 2 * hidden)],
        "mlp_out": [(0, 2, 0, row_count, 0, width + 2 * hidden, hidden)],
        "qkv": [(1, 0, HALF, row_count, 1, 0, width), (1, 0, 0, wide, 2, 0, 2 * width)],
    }
    early, late = ("attn_out", "in", "mlp_out"), ("qkv",)
    lefts = [own_left, own_first]
    other_lefts = [other_left, other_first]
    rights = [right, grad_queries, grad_wide]
    other_rights = [other_right, send_core(grad_queries), send_core(grad_wide)]

    def grads_of(names, ready):
        chosen = [product for name in names for product in parts[name]]
        used_left = sorted({product[0] for product in chosen})
        used_right = sorted({product[4] for product in chosen})
        products = [
            (used_left.index(p[0]), *p[1:4], used_right.index(p[4]), *p[5:]) for p in chosen
        ]
        first_left, _ = together((lefts[used_left[0]], ready))
        return partial_grads(
            [first_left] + [lefts[i] for i in used_left[1:]],
            [other_lefts[i] for i in used_left],
            [rights[i] for i in used_right],
            [other_rights[i] for i in used_right],
            products,
        )

    keep_rest, sent_rest = grads_of(early, grad_wide)
    got_rest = across_plane(sent_rest, 0)
    keep_qkv, sent_qkv = grads_of(late, keep_rest)
    grad_low, grad_high, _ = together((grad_low, grad_high, keep_qkv))
    above = send_along(grad_low, -1)
    below = send_along(grad_high, 1)
    got_rest, _ = together((got_rest, keep_qkv))
    begun = []
    for step in range(1, bits_of(blocks)):
        keep_rest, sent = halve(keep_rest, got_rest)
        begun.append(sent)
        got_rest = across_plane(sent, step)
    sent_qkv, _ = together((sent_qkv, begun))
    got_qkv = across_plane(sent_qkv, 0)
    sums_rest = by_plane(keep_rest, got_rest)
    landed_rest = z_sends(sums_rest)
    got_qkv, last = together((got_qkv, landed_rest[2]))
    landed_rest = landed_rest[:2] + [last] + landed_rest[3:]
    for step in range(1, bits_of(blocks)):
        keep_qkv, got_qkv = plane_step(keep_qkv, got_qkv, step)
    got_qkv, landed_rest = together((got_qkv, landed_rest))
    sums_qkv = by_plane(keep_qkv, got_qkv)
    landed_qkv = z_sends(sums_qkv)
    mine_rest = summed(landed_rest)
    above, below, _, _ = together((above, below, sums_qkv, mine_rest))
    mine_qkv = summed(landed_qkv)
    grad_inputs = input_grads(
        grad_queries, grad_own, below, above, inputs_low, grad_middle, qkv_pieces
    )
    sums = {}
    for names, total in ((early, spread(mine_rest)), (late, spread(mine_qkv))):
        first = 0
        for name in names:
            columns = sum(product[-1] for product in parts[name])
            sums[name] = total[:, first : first + columns]
            first += columns
    sum_qkv, sum_in = sums["qkv"], sums["in"]
    return (
        outputs[None],
        grad_inputs[None],
        sum_qkv * gain_one,
        sums["attn_out"],
        sum_in * gain_two,
        sums["mlp_out"].T,
        jnp.sum(sum_qkv * w_qkv.astype(F32), axis=1),
        jnp.sum(sum_in * w_in.astype(F32), axis=1),
    )


def solution(mesh):
    in_specs = (
        P("fsdp", "seq", None),
        P("fsdp", "seq", None),
        P("fsdp", None),
        P("fsdp", None),
        P("fsdp", None),
        P(None, "fsdp"),
        P("fsdp"),
        P("fsdp"),
    )
    out_specs = (
        P("fsdp", "seq", None),
        P("fsdp", "seq", None),
        P("fsdp", None),
        P("fsdp", None),
        P("fsdp", None),
        P(None, "fsdp"),
        P("fsdp"),
        P("fsdp"),
    )
    return jax.shard_map(
        on_device, mesh=mesh, in_specs=in_specs, out_specs=out_specs, check_vma=False
    )
```

```python
import functools

import jax
import jax.numpy as jnp
from jax import lax
from jax.experimental import pallas as pl
from jax.experimental.pallas import tpu as pltpu
from jax.sharding import PartitionSpec as P

HEADS = 12
HALF = 64
EPSILON = 1e-05
MASKED = -1e30
F32 = jnp.float32
BF16 = jnp.bfloat16


def dot(a, b, dims=((1,), (0,))):
    return lax.dot_general(a, b, (dims, ((), ())), preferred_element_type=F32)


def send_core(value):
    count = lax.axis_size("fsdp")
    return lax.ppermute(value, "fsdp", [(i, i ^ 1) for i in range(count)])


def send_z(value, step):
    count = lax.axis_size("fsdp")
    return lax.ppermute(value, "fsdp", [(i, i ^ (2 * step)) for i in range(count)])


def send_seq(value, step):
    count = lax.axis_size("seq")
    return lax.ppermute(value, "seq", [(i, i ^ step) for i in range(count)])


def send_along(value, step):
    count = lax.axis_size("seq")
    first, last = (max(0, -step), min(count, count - step))
    return lax.ppermute(value, "seq", [(i, i + step) for i in range(first, last)])


def bits_of(count):
    return count.bit_length() - 1


def column_cuts(width):
    parts = bits_of(lax.axis_size("seq"))
    tiles = width // 128
    edges = [(2 * r * tiles + parts) // (2 * parts) * 128 for r in range(parts)] + [width]
    return list(zip(edges[:-1], edges[1:]))


def direction(part, step):
    return 1 << ((part + step) % bits_of(lax.axis_size("seq")))


def along_z(mine):
    planes = lax.axis_size("fsdp") // 2
    return [send_z(mine, k) for k in range(1, planes)]


def by_range(along):
    return [
        jnp.stack([piece[:, first:last] for piece in along])
        for first, last in column_cuts(along[0].shape[1])
    ]


def across_plane(held, step):
    return [send_seq(value, direction(r, step)) for r, value in enumerate(held)]


def joined_ranges(held, got):
    return [jnp.concatenate(pair) for pair in zip(held, got)]


def across_rest_of_plane(held, got):
    for step in range(1, bits_of(lax.axis_size("seq"))):
        held = joined_ranges(held, got)
        got = across_plane(held, step)
    return held + got


def distances(part):
    found = [0]
    for step in range(bits_of(lax.axis_size("seq"))):
        found = found + [j ^ direction(part, step) for j in found]
    return found


def fits(n):
    return n % 8 == 0


def with_other_core(pieces):
    pieces = pieces + [send_core(piece) for piece in pieces]
    if fits(pieces[0].shape[1]):
        return pieces
    whole = sum(piece.size for piece in pieces)
    blocks, n, width = pieces[0].shape
    out = jnp.zeros((whole // (n * width), n, width), BF16)
    for to, first, last, source, index in placements(pieces, n, width):
        block = lax.dynamic_slice_in_dim(source, index, 1, 0)
        out = lax.dynamic_update_slice(out, block, (to, 0, first))
    return [out.reshape(-1, width)]


def placements(pieces, n, width):
    planes = lax.axis_size("fsdp") // 2
    blocks = lax.axis_size("seq")
    me, here = lax.axis_index("fsdp"), lax.axis_index("seq")
    plane, core = me // 2, me % 2
    half = len(pieces) // 2
    cuts = column_cuts(width)
    found = []
    for side in range(2):
        parity = core ^ side
        own, *others = pieces[side * half : (side + 1) * half]
        for j in range(blocks):
            found.append(((plane * 2 + parity) * blocks + j, 0, width, own, j))
        for r, (first, last) in enumerate(cuts):
            reach = distances(r)
            for m, j in enumerate(reach):
                late = m >= blocks // 2
                source = others[r + late * len(cuts)]
                for k in range(1, planes):
                    to = ((plane ^ k) * 2 + parity) * blocks + (here ^ j)
                    index = (m % (blocks // 2)) * (planes - 1) + k - 1
                    found.append((to, first, last, source, index))
    return found


def weight_scratch(pieces):
    if len(pieces) == 1:
        return []
    blocks, n, width = pieces[0].shape
    return [pltpu.VMEM((lax.axis_size("fsdp") * blocks, n, width), BF16)]


def whole_weight(sources, scratch):
    if not scratch:
        return sources[0][...]
    (out,) = scratch
    _, n, width = out.shape
    for to, first, last, source, index in placements(sources, n, width):
        out[to, :, first:last] = source[index]
    return out[...].reshape(-1, width)


def grads_kernel(counts, products, *refs):
    lefts, rights = counts
    own_a, other_a = refs[:lefts], refs[lefts : 2 * lefts]
    refs = refs[2 * lefts :]
    own_b, other_b = refs[:rights], refs[rights : 2 * rights]
    outs = refs[2 * rights :]
    blocks = lax.axis_size("seq")
    cuts = column_cuts(sum(product[-1] for product in products))
    start = 0
    for left, index, row, count, right, column, width in products:
        reach = slice(row, row + count)
        left_own, left_other = own_a[left][index, reach].T, other_a[left][index, reach].T
        rows = left_own.shape[0] // blocks
        for r, (low, high) in enumerate(cuts):
            keep, sent = outs[2 * r], outs[2 * r + 1]
            for first in range(max(low, start), min(high, start + width), 512):
                last = min(first + 512, high, start + width)
                lanes = slice(column + first - start, column + last - start)
                total = dot(left_own, own_b[right][:, lanes]) + dot(
                    left_other, other_b[right][:, lanes]
                )
                for m, j in enumerate(halving_order(r)):
                    out = sent if m >= blocks // 2 else keep
                    out[m % (blocks // 2), :, first - low : last - low] = total[
                        j * rows : (j + 1) * rows
                    ].astype(BF16)
        start += width


def halving_order(part):
    steps = bits_of(lax.axis_size("seq"))
    return [
        sum(direction(part, t) for t in range(steps) if m >> (steps - 1 - t) & 1)
        for m in range(1 << steps)
    ]


def partial_grads(own_a, other_a, own_b, other_b, products):
    blocks = lax.axis_size("seq")
    rows = own_a[0].shape[2] // blocks
    shapes = [
        jax.ShapeDtypeStruct((blocks // 2, rows, last - first), BF16)
        for first, last in column_cuts(sum(product[-1] for product in products))
        for _ in range(2)
    ]
    operands = [*own_a, *other_a, *own_b, *other_b]
    outs = pl.pallas_call(
        functools.partial(grads_kernel, (len(own_a), len(own_b)), products),
        out_shape=shapes,
        in_specs=[pl.BlockSpec(memory_space=pltpu.VMEM)] * len(operands),
        out_specs=[pl.BlockSpec(memory_space=pltpu.VMEM)] * len(shapes),
        compiler_params=pltpu.CompilerParams(vmem_limit_bytes=40 * 2**20),
        name="weight_grads",
    )(*operands)
    return list(outs[::2]), list(outs[1::2])


def halve_kernel(parts, *refs):
    for r in range(parts):
        keep, got = refs[r], refs[parts + r]
        low, high = refs[2 * parts + 2 * r], refs[2 * parts + 2 * r + 1]
        half = low.shape[0]
        low[...] = (keep[:half].astype(F32) + got[:half].astype(F32)).astype(BF16)
        high[...] = (keep[half:].astype(F32) + got[half:].astype(F32)).astype(BF16)


def halve(keep, got):
    parts = len(keep)
    shapes = [
        jax.ShapeDtypeStruct((value.shape[0] // 2,) + value.shape[1:], BF16)
        for value in keep
        for _ in range(2)
    ]
    outs = pl.pallas_call(
        functools.partial(halve_kernel, parts),
        out_shape=shapes,
        in_specs=[pl.BlockSpec(memory_space=pltpu.VMEM)] * (2 * parts),
        out_specs=[pl.BlockSpec(memory_space=pltpu.VMEM)] * (2 * parts),
        compiler_params=pltpu.CompilerParams(vmem_limit_bytes=40 * 2**20),
        name="add_and_halve",
    )(*keep, *got)
    return list(outs[::2]), list(outs[1::2])


def by_plane_kernel(parts, *refs):
    first = 0
    for r in range(parts):
        keep, got = refs[r], refs[parts + r]
        last = first + keep.shape[2]
        for k, out in enumerate(refs[2 * parts :]):
            out[:, first:last] = (keep[k].astype(F32) + got[k].astype(F32)).astype(BF16)
        first = last


def by_plane(keep, got):
    parts = len(keep)
    planes = lax.axis_size("fsdp") // 2
    keep = [value.reshape(planes, -1, value.shape[2]) for value in keep]
    got = [value.reshape(planes, -1, value.shape[2]) for value in got]
    shape = (keep[0].shape[1], sum(value.shape[2] for value in keep))
    return pl.pallas_call(
        functools.partial(by_plane_kernel, parts),
        out_shape=[jax.ShapeDtypeStruct(shape, BF16)] * planes,
        in_specs=[pl.BlockSpec(memory_space=pltpu.VMEM)] * (2 * parts),
        out_specs=[pl.BlockSpec(memory_space=pltpu.VMEM)] * planes,
        compiler_params=pltpu.CompilerParams(vmem_limit_bytes=40 * 2**20),
        name="add_by_plane",
    )(*keep, *got)


def plane_step(keep, got, step):
    keep, sent = halve(keep, got)
    return keep, across_plane(sent, step)


def z_sends(sums):
    return [sums[0]] + [send_z(value, k) for k, value in enumerate(sums) if k > 0]


def summed(landed):
    return functools.reduce(jnp.add, [piece.astype(F32) for piece in landed]).astype(BF16)


def spread(mine):
    blocks = lax.axis_size("seq")
    pieces = [mine] + [send_seq(mine, j) for j in range(1, blocks)]
    here = lax.axis_index("seq")
    rows = []
    for i in range(blocks):
        row = pieces[0]
        for j in range(1, blocks):
            row = jnp.where((here ^ j) == i, pieces[j], row)
        rows.append(row)
    return jnp.concatenate(rows, axis=0).astype(F32)


def row_order(width):
    planes = lax.axis_size("fsdp") // 2
    blocks = lax.axis_size("seq")
    n = width // (planes * 2 * blocks)
    me = lax.axis_index("fsdp")
    r = lax.broadcasted_iota(jnp.int32, (1, width), 1)
    i = r % n
    k = (r // n) % planes
    j = (r // (n * planes)) % blocks
    c = r // (n * planes * blocks)
    f = (((me // 2) ^ k) * 2) + ((me % 2) ^ c)
    natural = (f * blocks + (lax.axis_index("seq") ^ j)) * n + i
    d = lax.broadcasted_iota(jnp.int32, (width, width), 0)
    return (d == natural).astype(BF16)


def normalized(field):
    centered = field - jnp.mean(field, axis=-1, keepdims=True)
    inverse = lax.rsqrt(jnp.mean(centered * centered, axis=-1, keepdims=True) + EPSILON)
    return centered * inverse, inverse


def norm_back(grad_normal, normal, inverse):
    return inverse * (
        grad_normal
        - jnp.mean(grad_normal, axis=-1, keepdims=True)
        - normal * jnp.mean(grad_normal * normal, axis=-1, keepdims=True)
    )


def rope_tables(positions, head_dim):
    half_dim = head_dim // 2
    frequency = 10000.0 ** (-(2.0 * jnp.arange(half_dim, dtype=F32)) / head_dim)
    angles = positions.astype(F32)[:, None] * frequency[None, :]
    cosine, sine = jnp.cos(angles), jnp.sin(angles)
    return (
        jnp.concatenate([cosine] * 4, axis=1),
        jnp.concatenate([-sine, sine, -sine, sine], axis=1),
    )


def turned(pair, head_dim):
    lane = lax.broadcasted_iota(jnp.int32, pair.shape, 1)
    wide = pair.shape[1]
    half_dim = head_dim // 2
    return jnp.where(
        lane % head_dim < half_dim,
        pltpu.roll(pair, wide - half_dim, 1),
        pltpu.roll(pair, half_dim, 1),
    )


def attention_kernel(
    head_dim,
    count,
    before_ref,
    inputs_ref,
    after_ref,
    cosine_ref,
    sine_ref,
    *refs,
):
    first_ref, queries_ref, keys_ref, values_ref, probs_ref, attended_ref = refs[count : count + 6]
    weight = whole_weight(refs[:count], refs[count + 6 :])
    row_count, width = inputs_ref.shape
    wide = row_count + 2 * HALF
    pair = 2 * head_dim
    rows = jnp.concatenate([before_ref[...], inputs_ref[...], after_ref[...]], axis=0)
    normal, _ = normalized(rows.astype(F32))
    first_wide = normal.astype(BF16)
    first_in = first_wide[HALF : HALF + row_count]
    first_ref[...] = first_wide
    cosine, sine = cosine_ref[...], sine_ref[...]
    own_cosine, own_sine = (t[HALF : HALF + row_count] for t in (cosine, sine))
    here = lax.axis_index("seq")
    length = row_count * lax.axis_size("seq")
    first_key = here * row_count - HALF
    row = lax.broadcasted_iota(jnp.int32, (row_count, wide), 0)
    column = lax.broadcasted_iota(jnp.int32, (row_count, wide), 1)
    distance = column - HALF - row
    key_pos = first_key + column
    allowed = (key_pos >= 0) & (key_pos < length) & (jnp.abs(distance) <= HALF)
    low_lanes = lax.broadcasted_iota(jnp.int32, (row_count, pair), 1) < head_dim

    mixed_q = dot(first_in, weight[:, :width])
    mixed_k = dot(first_wide, weight[:, width : 2 * width])
    values_ref[...] = dot(first_wide, weight[:, 2 * width :]).astype(BF16)
    for p in range(width // pair):
        lanes = slice(p * pair, (p + 1) * pair)
        q = mixed_q[:, lanes]
        k = mixed_k[:, lanes]
        q = (q * own_cosine + turned(q, head_dim) * own_sine).astype(BF16)
        q = (q.astype(F32) * head_dim**-0.5).astype(BF16)
        k = (k * cosine + turned(k, head_dim) * sine).astype(BF16)
        queries_ref[:, lanes] = q
        keys_ref[:, lanes] = k
        v = values_ref[:, lanes]
        heads = []
        for side in range(2):
            mine = low_lanes if side == 0 else ~low_lanes
            scores = dot(jnp.where(mine, q, jnp.zeros_like(q)), k, ((1,), (1,)))
            scores = jnp.where(allowed, scores, MASKED)
            row_max = jnp.max(scores, axis=-1, keepdims=True)
            exponents = jnp.exp(scores - row_max)
            row_sum = jnp.sum(exponents, axis=-1, keepdims=True)
            weights = (exponents / row_sum).astype(BF16)
            probs_ref[2 * p + side] = weights
            heads.append(dot(weights, v))
        attended_ref[:, lanes] = jnp.where(low_lanes, heads[0], heads[1]).astype(BF16)


def attention_forward(before, inputs, after, cosine, sine, pieces, head_dim):
    row_count, width = inputs.shape
    wide = row_count + 2 * HALF
    heads = width // head_dim
    shapes = (
        (wide, width),
        (row_count, width),
        (wide, width),
        (wide, width),
        (heads, row_count, wide),
        (row_count, width),
    )
    return pl.pallas_call(
        functools.partial(attention_kernel, head_dim, len(pieces)),
        out_shape=[jax.ShapeDtypeStruct(shape, BF16) for shape in shapes],
        in_specs=[pl.BlockSpec(memory_space=pltpu.VMEM)] * (5 + len(pieces)),
        out_specs=[pl.BlockSpec(memory_space=pltpu.VMEM)] * 6,
        scratch_shapes=weight_scratch(pieces),
        compiler_params=pltpu.CompilerParams(vmem_limit_bytes=40 * 2**20),
        name="attention_forward",
    )(before, inputs, after, cosine, sine, *pieces)


def mlp_kernel(count, inputs_ref, attended_ref, cotangent_ref, order_ref, *refs):
    outputs_ref, grad_middle_ref, grad_attended_ref = refs[count : count + 3]
    right_ref, own_left_ref, sent_left_ref = refs[count + 3 : count + 6]
    weight = whole_weight(refs[:count], refs[count + 6 :])
    width = inputs_ref.shape[1]
    hidden = (weight.shape[1] - width) // 3
    attn_out = slice(0, width)
    into = slice(width, width + 2 * hidden)
    back = slice(width + 2 * hidden, width + 3 * hidden)
    transposed = ((1,), (1,))
    attended = attended_ref[...]
    middle = inputs_ref[...].astype(F32) + dot(attended, weight[:, attn_out])
    normal, inverse = normalized(middle)
    second_in = normal.astype(BF16)
    gate_up = dot(second_in, weight[:, into])
    gate, up = gate_up[:, :hidden], gate_up[:, hidden:]
    slope = (2.0 / jnp.pi) ** 0.5
    square = gate * gate
    level = jnp.tanh(slope * (gate + 0.044715 * gate * square))
    activated = 0.5 * gate * (1.0 + level)
    steep = 0.5 * (1.0 + level) + 0.5 * gate * (1.0 - level * level) * slope * (
        1.0 + 3 * 0.044715 * square
    )
    product = (activated * up).astype(BF16)
    outputs_ref[...] = (middle + dot(product, weight[:, back], transposed)).astype(BF16)
    grad_out = cotangent_ref[...]
    grad_product = dot(grad_out, weight[:, back])
    grad_gate_up = jnp.concatenate(
        [grad_product * up * steep, grad_product * activated], axis=1
    ).astype(BF16)
    grad_normal = dot(grad_gate_up, weight[:, into], transposed)
    grad_middle = grad_out.astype(F32) + norm_back(grad_normal, normal, inverse)
    grad_middle_ref[...] = grad_middle
    grad_attn_low = grad_middle.astype(BF16)
    grad_attended_ref[...] = dot(grad_attn_low, weight[:, attn_out], transposed).astype(BF16)
    right_ref[:, attn_out] = grad_attn_low
    right_ref[:, into] = grad_gate_up
    right_ref[:, back] = product
    depth = width // 2
    for x, left in enumerate((attended, second_in, grad_out)):
        moved = dot(left, order_ref[...]).astype(BF16)
        own_left_ref[x] = moved[:, :depth]
        sent_left_ref[x] = moved[:, depth:]


def mlp_both_ways(inputs, attended, cotangent, order, pieces):
    row_count, width = inputs.shape
    shapes = (
        ((row_count, width), BF16),
        ((row_count, width), F32),
        ((row_count, width), BF16),
        ((row_count, pieces[0].shape[-1]), BF16),
        ((3, row_count, width // 2), BF16),
        ((3, row_count, width // 2), BF16),
    )
    return pl.pallas_call(
        functools.partial(mlp_kernel, len(pieces)),
        out_shape=[jax.ShapeDtypeStruct(*shape) for shape in shapes],
        in_specs=[pl.BlockSpec(memory_space=pltpu.VMEM)] * (4 + len(pieces)),
        out_specs=[pl.BlockSpec(memory_space=pltpu.VMEM)] * 6,
        scratch_shapes=weight_scratch(pieces),
        compiler_params=pltpu.CompilerParams(vmem_limit_bytes=48 * 2**20),
        name="mlp_both_ways",
    )(inputs, attended, cotangent, order, *pieces)


def attention_back_kernel(
    head_dim,
    grad_ref,
    probs_ref,
    queries_ref,
    keys_ref,
    values_ref,
    cosine_ref,
    sine_ref,
    grad_queries_ref,
    wide_ref,
    own_ref,
    low_ref,
    high_ref,
):
    row_count, width = grad_ref.shape
    pair = 2 * head_dim
    cosine, sine = cosine_ref[...], sine_ref[...]
    own_cosine, own_sine = (t[HALF : HALF + row_count] for t in (cosine, sine))
    low_lanes = lax.broadcasted_iota(jnp.int32, (row_count, pair), 1) < head_dim
    over_rows = ((0,), (0,))

    def put(field, lanes):
        rounded = field.astype(BF16)
        wide_ref[:, lanes] = rounded
        low_ref[:, lanes] = rounded[:HALF]
        own_ref[:, lanes] = field[HALF : HALF + row_count]
        high_ref[:, lanes] = rounded[HALF + row_count :]

    for p in range(width // pair):
        lanes = slice(p * pair, (p + 1) * pair)
        grad, q = grad_ref[:, lanes], queries_ref[:, lanes]
        k, v = keys_ref[:, lanes], values_ref[:, lanes]
        grad_q, grad_k, grad_v = [], 0.0, 0.0
        for side in range(2):
            mine = low_lanes if side == 0 else ~low_lanes
            weights_low = probs_ref[2 * p + side]
            weights = weights_low.astype(F32)
            grad_mine = jnp.where(mine, grad, jnp.zeros_like(grad))
            q_mine = jnp.where(mine, q, jnp.zeros_like(q))
            grad_probs = dot(grad_mine, v, ((1,), (1,)))
            weighted = weights * grad_probs
            grad_scores = (
                weighted - weights * jnp.sum(weighted, axis=-1, keepdims=True)
            ).astype(BF16)
            grad_q.append(dot(grad_scores, k))
            grad_k = grad_k + dot(grad_scores, q_mine, over_rows)
            grad_v = grad_v + dot(weights_low, grad_mine, over_rows)
        turn = jnp.where(low_lanes, grad_q[0], grad_q[1]) * head_dim**-0.5
        grad_queries_ref[:, lanes] = (
            turn * own_cosine - turned(turn, head_dim) * own_sine
        ).astype(BF16)
        put(grad_k * cosine - turned(grad_k, head_dim) * sine, lanes)
        put(grad_v, slice(width + p * pair, width + (p + 1) * pair))


def attention_backward(grad, probs, queries, keys, values, cosine, sine, head_dim):
    row_count, width = grad.shape
    shapes = (
        ((row_count, width), BF16),
        ((row_count + 2 * HALF, 2 * width), BF16),
        ((row_count, 2 * width), F32),
        ((HALF, 2 * width), BF16),
        ((HALF, 2 * width), BF16),
    )
    return pl.pallas_call(
        functools.partial(attention_back_kernel, head_dim),
        out_shape=[jax.ShapeDtypeStruct(*shape) for shape in shapes],
        in_specs=[pl.BlockSpec(memory_space=pltpu.VMEM)] * 7,
        out_specs=[pl.BlockSpec(memory_space=pltpu.VMEM)] * len(shapes),
        compiler_params=pltpu.CompilerParams(vmem_limit_bytes=40 * 2**20),
        name="attention_backward",
    )(grad, probs, queries, keys, values, cosine, sine)


def input_grads_kernel(
    count, grad_queries_ref, own_ref, below_ref, above_ref, inputs_ref, middle_ref, *refs
):
    out_ref = refs[count]
    weight = whole_weight(refs[:count], refs[count + 1 :])
    row_count, width = inputs_ref.shape
    below, above = below_ref[...].astype(F32), above_ref[...].astype(F32)
    inner = jnp.zeros((row_count - HALF, below.shape[1]), F32)
    grad_kv = own_ref[...] + jnp.concatenate([below, inner]) + jnp.concatenate([inner, above])
    normal, inverse = normalized(inputs_ref[...].astype(F32))
    transposed = ((1,), (1,))
    grad_normal = dot(grad_queries_ref[...], weight[:, :width], transposed) + dot(
        grad_kv.astype(BF16), weight[:, width:], transposed
    )
    out_ref[...] = middle_ref[...] + norm_back(grad_normal, normal, inverse)


def input_grads(grad_queries, own, below, above, inputs, grad_middle, pieces):
    return pl.pallas_call(
        functools.partial(input_grads_kernel, len(pieces)),
        out_shape=jax.ShapeDtypeStruct(inputs.shape, F32),
        in_specs=[pl.BlockSpec(memory_space=pltpu.VMEM)] * (6 + len(pieces)),
        out_specs=pl.BlockSpec(memory_space=pltpu.VMEM),
        scratch_shapes=weight_scratch(pieces),
        compiler_params=pltpu.CompilerParams(vmem_limit_bytes=60 * 2**20),
        name="input_grads",
    )(grad_queries, own, below, above, inputs, grad_middle, *pieces)


def on_device(tokens, cotangent, w_qkv, w_attn_out, w_in, w_mlp_out, gain_attn, gain_mlp):
    row_count = tokens.shape[1]
    width = tokens.shape[2]
    head_dim = width // HEADS
    hidden = w_mlp_out.shape[0]
    blocks = lax.axis_size("seq")
    here = lax.axis_index("seq")
    n = w_qkv.shape[0] // blocks

    together = lax.optimization_barrier

    gain_one = gain_attn.astype(F32)[:, None]
    gain_two = gain_mlp.astype(F32)[:, None]

    def quarter(value):
        return lax.dynamic_slice_in_dim(value, here * n, n, 0)

    inputs_low = tokens[0]
    mine = (quarter(w_qkv).astype(F32) * quarter(gain_one)).astype(BF16)
    along = along_z(mine)
    order = row_order(width)
    key_pos = here * row_count - HALF + jnp.arange(row_count + 2 * HALF, dtype=jnp.int32)
    cosine, sine = rope_tables(key_pos, head_dim)
    before = send_along(inputs_low[row_count - HALF :], 1)
    after = send_along(inputs_low[:HALF], -1)
    along, before, after = together((along, before, after))
    held = by_range(along)
    got = across_plane(held, 0)
    rest = jnp.concatenate(
        [w_attn_out, (w_in.astype(F32) * gain_two).astype(BF16), w_mlp_out.T], axis=1
    )
    mine_rest, _ = together((quarter(rest), held))
    along_rest = along_z(mine_rest)
    across = across_rest_of_plane(held, got)

    own = (w_qkv.astype(F32) * gain_one).astype(BF16).reshape(blocks, n, -1)
    own, rest, along_rest, across = together((own, rest, along_rest, across))
    across, cosine, sine, order = together((across, cosine, sine, order))
    held_rest = by_range(along_rest)
    got_rest = across_plane(held_rest, 0)
    qkv_pieces = with_other_core([own] + across)
    first_wide, queries, keys, values, probs, attended = attention_forward(
        before, inputs_low, after, cosine, sine, qkv_pieces, head_dim
    )
    across_rest = across_rest_of_plane(held_rest, got_rest)
    rest_pieces = with_other_core([rest.reshape(blocks, n, -1)] + across_rest)
    outputs, grad_middle, grad_attended, right, own_left, sent_left = mlp_both_ways(
        inputs_low, attended, cotangent[0], order, rest_pieces
    )
    other_left, other_right = send_core(sent_left), send_core(right)
    moved = dot(first_wide, order).astype(BF16)
    own_first, sent_first = moved[None, :, : width // 2], moved[None, :, width // 2 :]
    other_first = send_core(sent_first)
    grad_queries, grad_wide, grad_own, grad_low, grad_high = attention_backward(
        grad_attended, probs, queries, keys, values, cosine, sine, head_dim
    )
    wide = row_count + 2 * HALF
    parts = {
        "attn_out": [(0, 0, 0, row_count, 0, 0, width)],
        "in": [(0, 1, 0, row_count, 0, width, 2 * hidden)],
        "mlp_out": [(0, 2, 0, row_count, 0, width + 2 * hidden, hidden)],
        "qkv": [(1, 0, HALF, row_count, 1, 0, width), (1, 0, 0, wide, 2, 0, 2 * width)],
    }
    early, late = ("attn_out", "in", "mlp_out"), ("qkv",)
    lefts = [own_left, own_first]
    other_lefts = [other_left, other_first]
    rights = [right, grad_queries, grad_wide]
    other_rights = [other_right, send_core(grad_queries), send_core(grad_wide)]

    def grads_of(names, ready):
        chosen = [product for name in names for product in parts[name]]
        used_left = sorted({product[0] for product in chosen})
        used_right = sorted({product[4] for product in chosen})
        products = [
            (used_left.index(p[0]), *p[1:4], used_right.index(p[4]), *p[5:]) for p in chosen
        ]
        first_left, _ = together((lefts[used_left[0]], ready))
        return partial_grads(
            [first_left] + [lefts[i] for i in used_left[1:]],
            [other_lefts[i] for i in used_left],
            [rights[i] for i in used_right],
            [other_rights[i] for i in used_right],
            products,
        )

    keep_rest, sent_rest = grads_of(early, grad_wide)
    got_rest = across_plane(sent_rest, 0)
    keep_qkv, sent_qkv = grads_of(late, keep_rest)
    grad_low, grad_high, _ = together((grad_low, grad_high, keep_qkv))
    above = send_along(grad_low, -1)
    below = send_along(grad_high, 1)
    got_rest, _ = together((got_rest, keep_qkv))
    begun = []
    for step in range(1, bits_of(blocks)):
        keep_rest, sent = halve(keep_rest, got_rest)
        begun.append(sent)
        got_rest = across_plane(sent, step)
    got_qkv = across_plane(sent_qkv, 0)
    sums_rest = by_plane(keep_rest, got_rest)
    landed_rest = z_sends(sums_rest)
    got_qkv, last = together((got_qkv, landed_rest[2]))
    landed_rest = landed_rest[:2] + [last] + landed_rest[3:]
    for step in range(1, bits_of(blocks)):
        keep_qkv, got_qkv = plane_step(keep_qkv, got_qkv, step)
    got_qkv, landed_rest = together((got_qkv, landed_rest))
    sums_qkv = by_plane(keep_qkv, got_qkv)
    landed_qkv = z_sends(sums_qkv)
    mine_rest = summed(landed_rest)
    above, below, _, _ = together((above, below, sums_qkv, mine_rest))
    mine_qkv = summed(landed_qkv)
    grad_inputs = input_grads(
        grad_queries, grad_own, below, above, inputs_low, grad_middle, qkv_pieces
    )
    sums = {}
    for names, total in ((early, spread(mine_rest)), (late, spread(mine_qkv))):
        first = 0
        for name in names:
            columns = sum(product[-1] for product in parts[name])
            sums[name] = total[:, first : first + columns]
            first += columns
    sum_qkv, sum_in = sums["qkv"], sums["in"]
    return (
        outputs[None],
        grad_inputs[None],
        sum_qkv * gain_one,
        sums["attn_out"],
        sum_in * gain_two,
        sums["mlp_out"].T,
        jnp.sum(sum_qkv * w_qkv.astype(F32), axis=1),
        jnp.sum(sum_in * w_in.astype(F32), axis=1),
    )


def solution(mesh):
    in_specs = (
        P("fsdp", "seq", None),
        P("fsdp", "seq", None),
        P("fsdp", None),
        P("fsdp", None),
        P("fsdp", None),
        P(None, "fsdp"),
        P("fsdp"),
        P("fsdp"),
    )
    out_specs = (
        P("fsdp", "seq", None),
        P("fsdp", "seq", None),
        P("fsdp", None),
        P("fsdp", None),
        P("fsdp", None),
        P(None, "fsdp"),
        P("fsdp"),
        P("fsdp"),
    )
    return jax.shard_map(
        on_device, mesh=mesh, in_specs=in_specs, out_specs=out_specs, check_vma=False
    )
```
